32 devices in a mesh: req: 4 (over y, x), hid: 8 (over z, core).
Axes of the slice: x: 2, y: 2, z: 4, core: 2. Of those that a mesh axis runs over, the one named last changes fastest.
Arguments:
- input_activations: bfloat16 [4, 512, 4096], P('req'), may hold values from -6 to 6
- prompt_extents: int32 [4], P('req'), may hold values from 1 to 512, as said below
- continuing_flags: int32 [4], P('req'), may hold values from 0 to 1, as said below
- owning_index: int32 [4], P('req'), may hold values from 0 to 7
- partition_arrangement: int32 [32], replicated, may hold values from 0 to 31, each once
- training_accept_pieces: float32 [4096, 4096], P(('req', 'hid')), may hold values from -0.09375 to 0.09375
- training_lookup_pieces: float32 [4096, 4096], P(('req', 'hid')), may hold values from -0.09375 to 0.09375
- training_content_pieces: float32 [4096, 4096], P(('req', 'hid')), may hold values from -0.09375 to 0.09375
- normalizer_scales: bfloat16 [2, 4096], replicated, may hold values from 0.5 to 1.5
- prior_step_blends: bfloat16 [7, 4096], replicated, may hold values from 0.049804688 to 0.94921875
- forgetting_bias_vector: float32 [4096], P('hid'), may hold values from -7 to -3
- forgetting_left_lowrank: bfloat16 [4096, 128], replicated, may hold values from -0.09375 to 0.09375
- forgetting_right_lowrank: bfloat16 [128, 4096], P(None, 'hid'), may hold values from -0.5 to 0.5
- instant_emphasis: float32 [4096], P('hid'), may hold values from -3 to 3
- group_normalizer_scale: float32 [4096], P('hid'), may hold values from 0.5 to 1.5
- gating_projection: bfloat16 [4096, 4096], P(None, 'hid'), may hold values from -0.09375 to 0.09375
- mixing_exit_projection: bfloat16 [4096, 4096], P('hid'), may hold values from -0.09375 to 0.09375
- kept_summary_places: float32 [4, 8, 64, 64, 64], P('req', 'hid'), may hold values from -6 to 6
- previous_normed_entries: bfloat16 [4, 2, 4096], P('req'), may hold values from -6 to 6
- feedforward_entry_proj: bfloat16 [14336, 4096], P(('req', 'hid')), may hold values from -0.09375 to 0.09375
- feedforward_exit_proj: bfloat16 [14336, 4096], P(('req', 'hid')), may hold values from -0.046875 to 0.046875
- feedforward_accept_proj: bfloat16 [4096, 4096], P(None, 'hid'), may hold values from -0.09375 to 0.09375
Outputs:
- layer_out: bfloat16 [4, 512, 4096], P('req', None, 'hid')
- new_states: float32 [4, 64, 64, 64], P('req', 'hid')
- new_shift: bfloat16 [4, 2, 4096], P('req')
The draws below stay inside these ranges and needn't reach their ends.
Inputs may be any that keep to these rules, and one draw needn't show every extreme that they name: `prompt_extents`: in every draw some request has length 512. `continuing_flags`: at least one request has 1 and at least one has 0. `owning_index`: read only where continuing_flags is 1. `partition_arrangement`: each of 0 to 31 appears once.
All inputs are finite; a program needn't handle non-finite values.
Results may differ from the reference program's by a relative error of at most 0.02.
Values may be sent and summed in bfloat16 or wider, within the bound.
No kernel may reach another device: no remote copies, remote signals or barrier semaphores. Data moves between devices by JAX's collectives and lax.ppermute only.
A program may use at most 256 MiB of HBM per device.

```python
from functools import partial
import jax
import jax.numpy as jnp
from jax import lax

EMBEDDING_DIM = 4096
ATTENTION_GROUPS = 64
GROUP_DIMENSION = 64
FF = 14336
RANK = 128
L = 512
REQS = 4
HOLDERS = 8
SHARDS = 32
BLK = 64
N_REQ = 4
N_HID = 8


def draw_prompt_extents(key, part):
    first_key, second_key = jax.random.split(jax.random.fold_in(key, 11))
    values = jax.random.randint(first_key, (REQS,), 1, L + 1)
    chosen = jax.random.randint(second_key, (), 0, REQS)
    return jnp.where(jnp.arange(REQS) == chosen, L, values).astype(jnp.int32)


def draw_continuing_flags(key, part):
    bits_key, first_key, second_key = jax.random.split(jax.random.fold_in(key, 37), 3)
    values = jax.random.randint(bits_key, (REQS,), 0, 2)
    forced_one = jax.random.randint(first_key, (), 0, REQS)
    forced_zero = (forced_one + 1 + jax.random.randint(second_key, (), 0, REQS - 1)) % REQS
    places = jnp.arange(REQS)
    values = jnp.where(places == forced_one, 1, values)
    values = jnp.where(places == forced_zero, 0, values)
    return values.astype(jnp.int32)


def touch_ends(array, own_key, smallest, top_value):
    spot = [jax.random.randint(jax.random.fold_in(own_key, axis), (), 0, length) for axis, length in enumerate(array.shape)]
    widest = array.shape.index(max(array.shape))
    neighbour = spot[:widest] + [(spot[widest] + 1) % array.shape[widest]] + spot[widest + 1:]
    return array.at[tuple(spot)].set(smallest).at[tuple(neighbour)].set(top_value)


def level_of(rng, dims, cuts, smallest, top_value):
    level = 1.0
    for dim, blocks in cuts:
        draws = jax.random.uniform(jax.random.fold_in(jax.random.fold_in(rng, 6), dim), (blocks,), jnp.float32, smallest / len(cuts), top_value / len(cuts))
        level = level * jnp.repeat(jnp.exp(draws), dims[dim] // blocks).reshape((-1,) + (1,) * (len(dims) - 1 - dim))
    return level


def gaussian(own_key, dims, scale, reach, cuts=(), dtype=jnp.bfloat16):
    level = level_of(own_key, dims, cuts, -0.22, 0.18) if cuts else 1.0
    entries = jax.random.normal(own_key, dims, jnp.float32) * scale * level
    return jnp.minimum(jnp.maximum(entries, -reach), reach).astype(dtype)


def setup_inputs(seed: int = 0) -> dict:
    arg_keys = jax.random.split(jax.random.key(seed), 23)
    return {
        "input_activations": gaussian(arg_keys[0], (REQS, L, EMBEDDING_DIM), 1.0, 6.0, ((0, 4),)),
        "prompt_extents": draw_prompt_extents(jax.random.fold_in(arg_keys[22], 71), 0),
        "continuing_flags": draw_continuing_flags(jax.random.fold_in(arg_keys[22], 71), 0),
        "owning_index": touch_ends(jax.random.randint(arg_keys[3], (REQS,), 0, HOLDERS), jax.random.fold_in(arg_keys[3], 1), 0, HOLDERS - 1).astype(jnp.int32),
        "partition_arrangement": jax.random.permutation(arg_keys[4], SHARDS).astype(jnp.int32),
        "training_accept_pieces": gaussian(arg_keys[5], (EMBEDDING_DIM, EMBEDDING_DIM), EMBEDDING_DIM ** -0.5, 0.09375, ((0, 32),), jnp.float32),
        "training_lookup_pieces": gaussian(arg_keys[6], (EMBEDDING_DIM, EMBEDDING_DIM), EMBEDDING_DIM ** -0.5, 0.09375, ((0, 32),), jnp.float32),
        "training_content_pieces": gaussian(arg_keys[7], (EMBEDDING_DIM, EMBEDDING_DIM), EMBEDDING_DIM ** -0.5, 0.09375, ((0, 32),), jnp.float32),
        "normalizer_scales": jnp.clip(1.0 + 0.1 * jax.random.normal(arg_keys[8], (2, EMBEDDING_DIM), jnp.float32), 0.5, 1.5).astype(jnp.bfloat16),
        "prior_step_blends": jnp.clip(jax.random.uniform(arg_keys[9], (7, EMBEDDING_DIM), jnp.float32, 0.049804688, 0.94921875), 0.049804688, 0.94921875).astype(jnp.bfloat16),
        "forgetting_bias_vector": jnp.clip(-7.0 + 4.0 * jax.random.uniform(arg_keys[10], (EMBEDDING_DIM,), jnp.float32) ** level_of(arg_keys[10], (EMBEDDING_DIM,), ((0, 8),), -0.2, 0.2), -7.0, -3.0),
        "forgetting_left_lowrank": gaussian(arg_keys[11], (EMBEDDING_DIM, RANK), EMBEDDING_DIM ** -0.5, 0.09375),
        "forgetting_right_lowrank": gaussian(arg_keys[12], (RANK, EMBEDDING_DIM), RANK ** -0.5, 0.5, ((1, 8),)),
        "instant_emphasis": gaussian(arg_keys[13], (EMBEDDING_DIM,), 0.5, 3.0, ((0, 8),), jnp.float32),
        "group_normalizer_scale": jnp.clip(1.0 + 0.1 * jax.random.normal(arg_keys[14], (EMBEDDING_DIM,), jnp.float32), 0.5, 1.5),
        "gating_projection": gaussian(arg_keys[15], (EMBEDDING_DIM, EMBEDDING_DIM), EMBEDDING_DIM ** -0.5, 0.09375, ((1, 8),)),
        "mixing_exit_projection": gaussian(arg_keys[16], (EMBEDDING_DIM, EMBEDDING_DIM), EMBEDDING_DIM ** -0.5, 0.09375, ((0, 8),)),
        "kept_summary_places": gaussian(arg_keys[17], (REQS, HOLDERS, ATTENTION_GROUPS, GROUP_DIMENSION, GROUP_DIMENSION), 1.0, 6.0, ((0, 4), (1, 8)), jnp.float32),
        "previous_normed_entries": gaussian(arg_keys[18], (REQS, 2, EMBEDDING_DIM), 1.0, 6.0, ((0, 4),)),
        "feedforward_entry_proj": gaussian(arg_keys[19], (FF, EMBEDDING_DIM), EMBEDDING_DIM ** -0.5, 0.09375, ((0, 32),)),
        "feedforward_exit_proj": gaussian(arg_keys[20], (FF, EMBEDDING_DIM), FF ** -0.5, 0.046875, ((0, 32),)),
        "feedforward_accept_proj": gaussian(arg_keys[21], (EMBEDDING_DIM, EMBEDDING_DIM), EMBEDDING_DIM ** -0.5, 0.09375, ((1, 8),)),
    }


def layer_norm(values, gain):
    center = values - lax.optimization_barrier(jnp.mean(values, axis=-1, keepdims=True))
    spread = lax.optimization_barrier(jnp.mean(center * center, axis=-1, keepdims=True))
    return center / jnp.sqrt(spread + 1e-05) * gain

def head_norm(outputs, gain_rows):
    center = outputs - lax.optimization_barrier(jnp.mean(outputs, axis=-1, keepdims=True))
    spread = lax.optimization_barrier(jnp.mean(center * center, axis=-1, keepdims=True))
    return center / jnp.sqrt(spread + 0.00064) * gain_rows

def shifted(values, first_row):
    return jnp.concatenate([first_row[None, :], values[:-1]], axis=0)

def rounded(values):
    return lax.optimization_barrier(values.astype(jnp.bfloat16)).astype(jnp.float32)

def segment_step(extra_diagonal_term, carried_summary, piece_sequence):
    acceptance_vectors, present_lookup_vectors, content_vectors, decays = piece_sequence
    inclusive = jnp.cumsum(decays, axis=0)
    exclusive = inclusive - decays
    closing = inclusive[-1]
    resulting_activations = jnp.einsum('thi,hij->thj', acceptance_vectors * jnp.exp(exclusive), carried_summary, precision=lax.Precision.HIGHEST)
    distance = exclusive[:, None] - inclusive[None, :]
    sizing = decays.shape[0]
    earlier = (jnp.arange(sizing)[:, None] > jnp.arange(sizing)[None, :]).astype(jnp.float32)
    factor = jnp.exp(jnp.minimum(distance, 0.0)) * earlier[:, :, None, None]
    scores = lax.optimization_barrier(jnp.sum(acceptance_vectors[:, None] * factor * present_lookup_vectors[None, :], axis=-1))
    resulting_activations = resulting_activations + jnp.einsum('tsh,shj->thj', scores, content_vectors, precision=lax.Precision.HIGHEST)
    resulting_activations = resulting_activations + lax.optimization_barrier(jnp.sum(acceptance_vectors * extra_diagonal_term * present_lookup_vectors, axis=-1, keepdims=True)) * content_vectors
    weighted = present_lookup_vectors * jnp.exp(closing[None] - inclusive)
    carried_summary = jnp.exp(closing)[:, :, None] * carried_summary + jnp.einsum('shi,shj->hij', weighted, content_vectors, precision=lax.Precision.HIGHEST)
    return (carried_summary, resulting_activations)

def reference(input_activations, prompt_extents, continuing_flags, owning_index, partition_arrangement, training_accept_pieces, training_lookup_pieces, training_content_pieces, normalizer_scales, prior_step_blends, forgetting_bias_vector, forgetting_left_lowrank, forgetting_right_lowrank, instant_emphasis, group_normalizer_scale, gating_projection, mixing_exit_projection, kept_summary_places, previous_normed_entries, feedforward_entry_proj, feedforward_exit_proj, feedforward_accept_proj):
    shard_rows = EMBEDDING_DIM // SHARDS
    server = rounded(jnp.stack([training_accept_pieces, training_lookup_pieces, training_content_pieces]))
    gain_rows = normalizer_scales.astype(jnp.float32)
    mix_rows = prior_step_blends.astype(jnp.float32)
    out_blocks = mixing_exit_projection.astype(jnp.float32).reshape(N_HID, EMBEDDING_DIM // N_HID, EMBEDDING_DIM)
    value_sets = feedforward_exit_proj.astype(jnp.float32).reshape(N_REQ, N_HID, FF // SHARDS, EMBEDDING_DIM)
    key_table = feedforward_entry_proj.astype(jnp.float32)
    recept_table = feedforward_accept_proj.astype(jnp.float32)
    positions = jnp.arange(L)
    segment_cursor = partial(segment_step, instant_emphasis.reshape(ATTENTION_GROUPS, GROUP_DIMENSION))

    def by_blocks(values):
        return values.reshape(L // BLK, BLK, ATTENTION_GROUPS, GROUP_DIMENSION)

    def per_request(inputs):
        token_rows, length, resuming, slot, saved, carry_rows = inputs
        present = positions < length
        carried = carry_rows.astype(jnp.float32)
        normed_in = layer_norm(token_rows.astype(jnp.float32), gain_rows[0])
        before = shifted(normed_in, jnp.where(resuming == 1, carried[0], 0.0))
        blended = (normed_in[None] + (before - normed_in)[None] * mix_rows[:5, None, :]).astype(jnp.bfloat16)
        permuted = jnp.take(blended[:3].reshape(3, L, SHARDS, shard_rows), partition_arrangement, axis=2).reshape(3, L, EMBEDDING_DIM)
        projected = jnp.einsum('mtd,mdc->mtc', permuted.astype(jnp.float32), server, precision=lax.Precision.HIGHEST)
        low_rank = jnp.tanh(jnp.dot(blended[3], forgetting_left_lowrank, preferred_element_type=jnp.float32)).astype(jnp.bfloat16)
        log_decay = -jnp.exp(forgetting_bias_vector + jnp.dot(low_rank, forgetting_right_lowrank, preferred_element_type=jnp.float32))
        log_decay = jnp.where(present[:, None], log_decay, 0.0)
        gate = jax.nn.silu(jnp.dot(blended[4], gating_projection, preferred_element_type=jnp.float32))
        present_lookup_vectors = jnp.where(present[:, None], projected[1], 0.0)
        carried_summary = jnp.where(resuming == 1, lax.dynamic_index_in_dim(saved, slot, 0, keepdims=False), 0.0)
        carried_summary, outputs = lax.scan(segment_cursor, carried_summary, (by_blocks(projected[0]), by_blocks(present_lookup_vectors), by_blocks(projected[2]), by_blocks(log_decay)))
        grouped = head_norm(outputs.reshape(L, ATTENTION_GROUPS, GROUP_DIMENSION), group_normalizer_scale.reshape(ATTENTION_GROUPS, GROUP_DIMENSION)).reshape(L, EMBEDDING_DIM)
        gated = (grouped * gate).astype(jnp.bfloat16)
        head_sets = gated.astype(jnp.float32).reshape(L, N_HID, EMBEDDING_DIM // N_HID)
        partials = jnp.einsum('lnc,ncd->nld', head_sets, out_blocks, precision=lax.Precision.HIGHEST)
        attended = lax.optimization_barrier(jnp.sum(rounded(partials), axis=0))
        middle = (token_rows.astype(jnp.float32) + attended).astype(jnp.bfloat16)
        chan_in = layer_norm(middle.astype(jnp.float32), gain_rows[1])
        chan_before = shifted(chan_in, jnp.where(resuming == 1, carried[1], 0.0))
        chan_mixed = (chan_in[None] + (chan_before - chan_in)[None] * mix_rows[5:, None, :]).astype(jnp.bfloat16)
        inner = jnp.dot(chan_mixed[0].astype(jnp.float32), key_table.T, precision=lax.Precision.HIGHEST)
        hidden = jnp.square(jnp.maximum(inner, 0.0)).astype(jnp.bfloat16)
        partial_sets = jnp.einsum('lgnu,gnud->nld', hidden.astype(jnp.float32).reshape(L, N_REQ, N_HID, FF // SHARDS), value_sets, precision=lax.Precision.HIGHEST)
        summed = lax.optimization_barrier(jnp.sum(rounded(partial_sets), axis=0))
        gate_rows = jax.nn.sigmoid(jnp.dot(chan_mixed[1].astype(jnp.float32), recept_table, precision=lax.Precision.HIGHEST))
        combined = middle.astype(jnp.float32) + gate_rows * summed
        layer_row = jnp.where(present[:, None], combined, 0.0).astype(jnp.bfloat16)
        last_index = length - 1
        shift_out = jnp.stack([lax.dynamic_index_in_dim(normed_in, last_index, 0, keepdims=False), lax.dynamic_index_in_dim(chan_in, last_index, 0, keepdims=False)]).astype(jnp.bfloat16)
        return (layer_row, carried_summary, shift_out)
    layer_out, new_states, new_shift = lax.map(per_request, (input_activations, prompt_extents, continuing_flags, owning_index, kept_summary_places, previous_normed_entries))
    return (layer_out, new_states, new_shift)
```

```python
from functools import partial

import jax
import jax.numpy as jnp
from jax import lax
from jax.experimental import pallas as pl
from jax.experimental.pallas import tpu as pltpu
from jax.sharding import PartitionSpec as P

GROUP_DIMENSION = 64
PAIR = 2 * GROUP_DIMENSION
CHUNK = 64
BF16 = jnp.bfloat16
F32 = jnp.float32


def layer_norm(values, gain):
    center = values - jnp.mean(values, axis=-1, keepdims=True)
    spread = jnp.mean(center * center, axis=-1, keepdims=True)
    return center / jnp.sqrt(spread + 1e-05) * gain


def shifted(values, first_row):
    return jnp.concatenate([first_row[None, :], values[:-1]], axis=0)


def matmul(a, b):
    return jnp.dot(a, b, preferred_element_type=F32)


def matmul_nt(a, b):
    return lax.dot_general(a, b, (((1,), (1,)), ((), ())), preferred_element_type=F32)


def matmul_tn(a, b):
    return lax.dot_general(a, b, (((0,), (0,)), ((), ())), preferred_element_type=F32)


class Exchange:
    WINDOW = 3

    def __init__(self, req):
        self.req = req
        self.sent = {1: [], 2: []}

    def send(self, value, axis):
        past = self.sent[axis]
        if len(past) >= self.WINDOW:
            value, _ = lax.optimization_barrier((value, past[-self.WINDOW]))
        got = lax.ppermute(value, "req", [(i, i ^ axis) for i in range(4)])
        past.append(got)
        return got

    def near(self, value):
        return {0: value, 1: self.send(value, 1), 2: self.send(value, 2)}

    def far(self, pieces, axis):
        pieces[3] = self.send(pieces[3 - axis], axis)

    def whole(self, value):
        blocks = lax.all_gather(value, "req", axis=0, tiled=False)
        me = lax.axis_index("req")
        return {
            d: lax.dynamic_index_in_dim(blocks, me ^ d, 0, keepdims=False)
            for d in range(self.req)
        }


def by_head(values, first_lanes):
    zeros = jnp.zeros_like(values)
    return jnp.concatenate(
        [jnp.where(first_lanes, values, zeros), jnp.where(first_lanes, zeros, values)], axis=0
    )


def split_matmul(values, weights):
    high = values.astype(BF16)
    low = (values - high.astype(F32)).astype(BF16)
    return matmul(high, weights) + matmul(low, weights)


def recurrence_kernel(
    length_ref,
    rec_ref,
    key_ref,
    val_ref,
    decay_ref,
    gate_ref,
    bias_ref,
    bonus_ref,
    gain_ref,
    start_ref,
    gated_ref,
    state_ref,
    held,
):
    length = length_ref[0]
    tokens = rec_ref.shape[0]
    size = min(CHUNK, tokens)
    lanes = lax.broadcasted_iota(jnp.int32, (size, PAIR), 1)
    first_lanes = lanes < GROUP_DIMENSION
    row_of = lax.broadcasted_iota(jnp.int32, (size, PAIR), 0)
    t_of = lax.broadcasted_iota(jnp.int32, (size, 2 * size), 0)
    s_of = lax.broadcasted_iota(jnp.int32, (size, 2 * size), 1) & (size - 1)
    side_a = lax.broadcasted_iota(jnp.int32, (PAIR, PAIR), 0) < GROUP_DIMENSION
    side_b = lax.broadcasted_iota(jnp.int32, (PAIR, PAIR), 1) < GROUP_DIMENSION
    own_head = side_a == side_b
    average = jnp.where(own_head, 1.0 / GROUP_DIMENSION, 0.0).astype(BF16)
    start = start_ref[...].reshape(PAIR, GROUP_DIMENSION)
    held[...] = jnp.where(own_head, jnp.concatenate([start, start], axis=1), 0.0).T
    bias = bias_ref[...]
    bonus = bonus_ref[...]
    gain = gain_ref[...]
    for index in range(tokens // size):
        rows = pl.ds(index * size, size)
        present = row_of + index * size < length
        rec = rec_ref[rows, :]
        key = jnp.where(present, key_ref[rows, :], 0.0)
        val = val_ref[rows, :].astype(BF16)
        total = jnp.where(present, -jnp.exp(bias + decay_ref[rows, :]), 0.0)
        scores = jnp.where(
            t_of == s_of,
            matmul_nt((rec * bonus).astype(BF16), by_head(key.astype(BF16), first_lanes)),
            0.0,
        )
        before = jnp.zeros_like(total)
        after = jnp.zeros_like(total)
        span = 1
        while span < size:
            later = (row_of & span) != 0
            scaled = (jnp.where(later, rec, key) * jnp.exp(jnp.where(later, before, after))).astype(
                BF16
            )
            pairs = matmul_nt(scaled, by_head(scaled, first_lanes))
            chosen = (
                ((t_of & span) != 0)
                & ((s_of & span) == 0)
                & ((t_of & (-2 * span)) == (s_of & (-2 * span)))
            )
            scores = jnp.where(chosen, pairs, scores)
            partner = jnp.where(
                later, pltpu.roll(total, span, 0), pltpu.roll(total, size - span, 0)
            )
            before = before + jnp.where(later, partner, 0.0)
            after = after + jnp.where(later, 0.0, partner)
            total = total + partner
            span *= 2
        state = held[...]
        out = matmul(scores.astype(BF16), by_head(val, first_lanes))
        out = out + matmul_nt((rec * jnp.exp(before)).astype(BF16), state.astype(BF16))
        update = matmul_tn(val, (key * jnp.exp(after)).astype(BF16))
        held[...] = state * jnp.exp(total[:1, :]) + jnp.where(own_head, update, 0.0)
        center = out - split_matmul(out, average)
        spread = split_matmul(center * center, average)
        grouped = center * lax.rsqrt(spread + 0.00064) * gain
        gate = gate_ref[rows, :]
        gated_ref[rows, :] = (grouped * (gate / (1.0 + jnp.exp(-gate)))).astype(BF16)
    final = held[...].T
    state_ref[...] = (final[:, :GROUP_DIMENSION] + final[:, GROUP_DIMENSION:]).reshape(
        state_ref.shape
    )


def recurrence(length, rec, key, val, decay, gate, bias, bonus, gain, start):
    tokens, width = rec.shape
    wide = pl.BlockSpec((tokens, PAIR), lambda p: (0, p))
    row = pl.BlockSpec((1, PAIR), lambda p: (0, p))
    states = pl.BlockSpec((2, GROUP_DIMENSION, GROUP_DIMENSION), lambda p: (p, 0, 0))
    return pl.pallas_call(
        recurrence_kernel,
        grid=(width // PAIR,),
        in_specs=[pl.BlockSpec(memory_space=pltpu.SMEM)] + [wide] * 5 + [row] * 3 + [states],
        out_specs=[wide, states],
        out_shape=[
            jax.ShapeDtypeStruct((tokens, width), BF16),
            jax.ShapeDtypeStruct(start.shape, F32),
        ],
        scratch_shapes=[pltpu.VMEM((PAIR, PAIR), F32)],
        compiler_params=pltpu.CompilerParams(vmem_limit_bytes=24 << 20),
        cost_estimate=pl.CostEstimate(
            flops=tokens * width * 4096, bytes_accessed=tokens * width * 22, transcendentals=0
        ),
        name="recurrence",
    )(length, rec, key, val, decay, gate, bias, bonus, gain, start)


def prepare_kernel(
    order_ref,
    length_ref,
    tokens_ref,
    gain_ref,
    first_ref,
    mix_ref,
    out0_ref,
    out1_ref,
    out2_ref,
    out3_ref,
    out4_ref,
    last_ref,
    mean_ref,
    root_ref,
):
    step = pl.program_id(0)
    block = out0_ref.shape[1]
    seq_len, width = tokens_ref.shape

    @pl.when(step == 0)
    def _():
        count = min(64, seq_len)
        for index in range(seq_len // count):
            rows = pl.ds(index * count, count)
            values = tokens_ref[rows, :].astype(F32)
            mean = jnp.mean(values, axis=1, keepdims=True)
            center = values - mean
            spread = jnp.mean(center * center, axis=1, keepdims=True)
            mean_ref[rows, :] = jnp.broadcast_to(mean, (count, 128))
            root_ref[rows, :] = jnp.broadcast_to(lax.rsqrt(spread + 1e-05), (count, 128))

    columns = pl.ds(pl.multiple_of(order_ref[step] * block, block), block)
    values = tokens_ref[:, columns].astype(F32)
    normed = (values - mean_ref[:, :1]) * root_ref[:, :1] * gain_ref[:1, columns]
    places = lax.broadcasted_iota(jnp.int32, normed.shape, 0)
    before = jnp.where(places == 0, first_ref[:1, columns], pltpu.roll(normed, 1, 0))
    change = before - normed
    for m, out_ref in enumerate((out0_ref, out1_ref, out2_ref, out3_ref, out4_ref)):
        out_ref[...] = (normed + change * mix_ref[m : m + 1, columns]).astype(BF16)
    last = places == length_ref[0] - 1
    last_ref[...] = jnp.sum(jnp.where(last, normed, 0.0), axis=0, keepdims=True)


def prepare(order, length, tokens, gain, first, mixes):
    seq_len, width = tokens.shape
    blocks = order.shape[0]
    block = width // blocks

    def rows(count):
        return pl.BlockSpec((count, width), lambda j, *_: (0, 0))

    moved = pl.BlockSpec((seq_len, block), lambda j, *_: (0, j))
    natural = pl.BlockSpec((seq_len, block), lambda j, order, *_: (0, order[j]))
    return pl.pallas_call(
        prepare_kernel,
        grid_spec=pltpu.PrefetchScalarGridSpec(
            num_scalar_prefetch=2,
            grid=(blocks,),
            in_specs=[rows(seq_len), rows(1), rows(1), rows(mixes.shape[0])],
            out_specs=[moved] * 3
            + [natural] * 2
            + [pl.BlockSpec((1, block), lambda j, order, *_: (0, order[j]))],
            scratch_shapes=[pltpu.VMEM((seq_len, 128), F32)] * 2,
        ),
        out_shape=[jax.ShapeDtypeStruct((seq_len, width), BF16)] * 5
        + [jax.ShapeDtypeStruct((1, width), F32)],
        compiler_params=pltpu.CompilerParams(vmem_limit_bytes=32 << 20),
        cost_estimate=pl.CostEstimate(
            flops=seq_len * width * 20, bytes_accessed=seq_len * width * 12, transcendentals=0
        ),
        name="prepare",
    )(order, length, tokens, gain, first, mixes)


def exit_kernel(count, *refs):
    hidden, values, out_ref = refs[:count], refs[count : 2 * count], refs[-1]
    total = matmul(hidden[0][...], values[0][...])
    for h, v in zip(hidden[1:], values[1:]):
        total = total + matmul(h[...], v[...])
    out_ref[...] = total.astype(BF16)


def exit_product(hidden, values):
    tokens = hidden[0].shape[0]
    width = values[0].shape[1]
    tile = min(512, width)
    return pl.pallas_call(
        partial(exit_kernel, len(hidden)),
        grid=(width // tile,),
        in_specs=[pl.BlockSpec(h.shape, lambda n: (0, 0)) for h in hidden]
        + [pl.BlockSpec((v.shape[0], tile), lambda n: (0, n)) for v in values],
        out_specs=pl.BlockSpec((tokens, tile), lambda n: (0, n)),
        out_shape=jax.ShapeDtypeStruct((tokens, width), BF16),
        compiler_params=pltpu.CompilerParams(vmem_limit_bytes=32 << 20),
        cost_estimate=pl.CostEstimate(
            flops=2 * tokens * width * sum(h.shape[1] for h in hidden),
            bytes_accessed=2 * width * (tokens + sum(v.shape[0] for v in values)),
            transcendentals=0,
        ),
        name="exit_product",
    )(*hidden, *values)


def local(
    input_activations,
    prompt_extents,
    continuing_flags,
    owning_index,
    partition_arrangement,
    training_accept_pieces,
    training_lookup_pieces,
    training_content_pieces,
    normalizer_scales,
    prior_step_blends,
    forgetting_bias_vector,
    forgetting_left_lowrank,
    forgetting_right_lowrank,
    instant_emphasis,
    group_normalizer_scale,
    gating_projection,
    mixing_exit_projection,
    kept_summary_places,
    previous_normed_entries,
    feedforward_entry_proj,
    feedforward_exit_proj,
    feedforward_accept_proj,
):
    hid = lax.axis_size("hid")
    req = lax.axis_size("req")
    here = lax.axis_index("req")
    slot = lax.axis_index("hid")
    token_rows = input_activations[0]
    seq_len, width = token_rows.shape
    local_width = mixing_exit_projection.shape[0]
    heads = local_width // GROUP_DIMENSION
    shards = partition_arrangement.shape[0]
    shard_rows = width // shards
    length = prompt_extents[0]
    resuming = continuing_flags[0]
    present = jnp.arange(seq_len) < length

    owned = (resuming == 1) & (owning_index[0] == slot)
    saved = jnp.where(owned, kept_summary_places[0, 0].astype(BF16), 0)
    start = lax.psum_scatter(
        saved.reshape(saved.shape[0], -1), "hid", scatter_dimension=0, tiled=True
    )
    start = start.astype(F32).reshape(heads, GROUP_DIMENSION, GROUP_DIMENSION)

    order = jnp.concatenate(
        [
            lax.dynamic_slice_in_dim(partition_arrangement, (here ^ d) * hid, hid, 0)
            for d in range(req)
        ]
    )
    gain_rows = normalizer_scales.astype(F32)
    mix_rows = prior_step_blends.astype(F32)
    carried = jnp.where(resuming == 1, previous_normed_entries[0].astype(F32), 0.0)
    if shard_rows % 128 == 0:
        *blended, last_in = prepare(
            order, prompt_extents, token_rows, gain_rows[:1], carried[:1], mix_rows[:5]
        )
    else:
        normed_in = layer_norm(token_rows.astype(F32), gain_rows[0])
        before = shifted(normed_in, carried[0])
        blended = [
            (normed_in + (before - normed_in) * mix_rows[m][None, :]).astype(BF16)
            for m in range(5)
        ]
        for m in range(3):
            blocks = blended[m].reshape(seq_len, shards, shard_rows)
            blended[m] = jnp.take(blocks, order, axis=1).reshape(seq_len, width)
        last_in = lax.dynamic_slice_in_dim(normed_in, length - 1, 1, 0)
    low_rank = jnp.tanh(matmul(blended[3], forgetting_left_lowrank)).astype(BF16)
    decay = matmul(low_rank, forgetting_right_lowrank)
    gate = matmul(blended[4], gating_projection)

    exchange = Exchange(req)
    rows_here = feedforward_entry_proj.shape[0]
    half = rows_here // 2
    key_halves = [feedforward_entry_proj[:half], feedforward_entry_proj[half:]]
    parts = 2
    wide = local_width // parts
    split_values = feedforward_exit_proj.reshape(rows_here, hid, parts, wide)
    value_halves = [
        [
            split_values[first : first + half, :, part].reshape(half, hid * wide)
            for first in (0, half)
        ]
        for part in range(parts)
    ]
    mine = []
    for pieces in (training_lookup_pieces, training_content_pieces, training_accept_pieces):
        blocks = pieces.astype(BF16).reshape(shard_rows, hid, local_width).transpose(1, 0, 2)
        if mine:
            blocks, _ = lax.optimization_barrier((blocks, mine[-1]))
        mine.append(lax.all_to_all(blocks, "hid", split_axis=0, concat_axis=0, tiled=True))
    trainer_halves = [
        jnp.split(blocks.reshape(hid * shard_rows, local_width), 2, axis=0) for blocks in mine
    ]
    if req == 4:
        near, far = exchange.near, exchange.far
        key_rows = [near(key_halves[0])]
        trained = [[near(block) for block in trainer_halves[0]]]
        trained.append([near(block) for block in trainer_halves[1]])
        far(trained[0][0], 2)
        far(trained[0][1], 1)
        trained.append([near(block) for block in trainer_halves[2]])
        for m in (1, 2):
            far(trained[m][0], 2)
            far(trained[m][1], 1)
        key_rows.append(near(key_halves[1]))
        far(key_rows[0], 2)
        far(key_rows[1], 1)
        value_rows = []
        for part in range(parts):
            value_rows.append([near(block) for block in value_halves[part]])
            far(value_rows[part][0], 2)
            far(value_rows[part][1], 1)
    else:
        key_rows = [exchange.whole(block) for block in key_halves]
        trained = [[exchange.whole(block) for block in blocks] for blocks in trainer_halves]
        value_rows = [[exchange.whole(block) for block in blocks] for blocks in value_halves]

    half_span = hid * shard_rows // 2

    def project(values, halves):
        total = 0.0
        for d in range(req):
            for side in range(2):
                first = (2 * d + side) * half_span
                total = total + matmul(values[:, first : first + half_span], halves[side][d])
        return total

    key, val, rec = (project(blended[m], trained[at]) for at, m in enumerate((1, 2, 0)))
    gated, new_state = recurrence(
        prompt_extents,
        rec,
        key,
        val,
        decay,
        gate,
        forgetting_bias_vector[None],
        instant_emphasis[None],
        group_normalizer_scale[None],
        start,
    )
    head_terms = matmul(gated, mixing_exit_projection).astype(BF16)
    attended = lax.psum(head_terms, "hid").astype(F32)
    middle = (token_rows.astype(F32) + attended).astype(BF16)
    mid_share = lax.dynamic_slice_in_dim(middle, slot * local_width, local_width, 1)
    chan_in = layer_norm(middle.astype(F32), gain_rows[1])
    chan_before = shifted(chan_in, carried[1])
    chan_mixed = [
        (chan_in + (chan_before - chan_in) * mix_rows[5 + m][None, :]).astype(BF16)
        for m in range(2)
    ]
    gate_rows = jax.nn.sigmoid(matmul(chan_mixed[1], feedforward_accept_proj))
    hidden = [
        jnp.square(jnp.maximum(matmul_nt(chan_mixed[0], key_rows[side][d]), 0.0)).astype(BF16)
        for d in range(req)
        for side in range(2)
    ]
    summed = []
    for part in range(parts):
        terms = exit_product(
            hidden, [value_rows[part][side][d] for d in range(req) for side in range(2)]
        )
        summed.append(lax.psum_scatter(terms, "hid", scatter_dimension=1, tiled=True))
    mixed_out = jnp.concatenate(summed, axis=1).astype(F32)
    combined = mid_share.astype(F32) + gate_rows * mixed_out
    layer_out = jnp.where(present[:, None], combined, 0.0).astype(BF16)[None]
    last_chan = lax.dynamic_slice_in_dim(chan_in, length - 1, 1, 0)
    shift_out = jnp.concatenate([last_in, last_chan]).astype(BF16)[None]
    return (layer_out, new_state[None], shift_out)


def solution(mesh):
    placed = (
        P("req", None, None),
        P("req"),
        P("req"),
        P("req"),
        P(),
        P(("req", "hid"), None),
        P(("req", "hid"), None),
        P(("req", "hid"), None),
        P(),
        P(),
        P("hid"),
        P(),
        P(None, "hid"),
        P("hid"),
        P("hid"),
        P(None, "hid"),
        P("hid", None),
        P("req", "hid", None, None, None),
        P("req", None, None),
        P(("req", "hid"), None),
        P(("req", "hid"), None),
        P(None, "hid"),
    )
    return jax.shard_map(
        local,
        mesh=mesh,
        in_specs=placed,
        out_specs=(P("req", None, "hid"), P("req", "hid", None, None), P("req", None, None)),
        check_vma=False,
    )
```

```python
from functools import partial

import jax
import jax.numpy as jnp
from jax import lax
from jax.experimental import pallas as pl
from jax.experimental.pallas import tpu as pltpu
from jax.sharding import PartitionSpec as P

GROUP_DIMENSION = 64
PAIR = 2 * GROUP_DIMENSION
CHUNK = 64
BF16 = jnp.bfloat16
F32 = jnp.float32
MICROSECOND = 3690000
VMEM_BYTES = 60 << 20


def layer_norm(values, gain):
    center = values - jnp.mean(values, axis=-1, keepdims=True)
    spread = jnp.mean(center * center, axis=-1, keepdims=True)
    return center / jnp.sqrt(spread + 1e-05) * gain


def shifted(values, first_row):
    return jnp.concatenate([first_row[None, :], values[:-1]], axis=0)


def matmul(a, b):
    return jnp.dot(a, b, preferred_element_type=F32)


def matmul_nt(a, b):
    return lax.dot_general(a, b, (((1,), (1,)), ((), ())), preferred_element_type=F32)


def matmul_tn(a, b):
    return lax.dot_general(a, b, (((0,), (0,)), ((), ())), preferred_element_type=F32)


def across(value, axis):
    return lax.ppermute(value, "req", [(i, i ^ axis) for i in range(4)])


def whole(value, req):
    blocks = lax.all_gather(value, "req", axis=0, tiled=False)
    me = lax.axis_index("req")
    return [lax.dynamic_index_in_dim(blocks, me ^ d, 0, keepdims=False) for d in range(req)]


def by_head(values, first_lanes):
    zeros = jnp.zeros_like(values)
    return jnp.concatenate(
        [jnp.where(first_lanes, values, zeros), jnp.where(first_lanes, zeros, values)], axis=0
    )


def split_matmul(values, weights):
    high = values.astype(BF16)
    low = (values - high.astype(F32)).astype(BF16)
    return matmul(high, weights) + matmul(low, weights)


def recurrence_kernel(
    length_ref,
    rec_ref,
    key_ref,
    val_ref,
    decay_ref,
    gate_ref,
    bias_ref,
    bonus_ref,
    gain_ref,
    start_ref,
    gated_ref,
    state_ref,
    held,
):
    length = length_ref[0]
    tokens = rec_ref.shape[0]
    size = min(CHUNK, tokens)
    lanes = lax.broadcasted_iota(jnp.int32, (size, PAIR), 1)
    first_lanes = lanes < GROUP_DIMENSION
    row_of = lax.broadcasted_iota(jnp.int32, (size, PAIR), 0)
    t_of = lax.broadcasted_iota(jnp.int32, (size, 2 * size), 0)
    s_of = lax.broadcasted_iota(jnp.int32, (size, 2 * size), 1) & (size - 1)
    side_a = lax.broadcasted_iota(jnp.int32, (PAIR, PAIR), 0) < GROUP_DIMENSION
    side_b = lax.broadcasted_iota(jnp.int32, (PAIR, PAIR), 1) < GROUP_DIMENSION
    own_head = side_a == side_b
    average = jnp.where(own_head, 1.0 / GROUP_DIMENSION, 0.0).astype(BF16)
    pairs_here = rec_ref.shape[1] // PAIR
    for pair in range(pairs_here):
        start = start_ref[2 * pair : 2 * pair + 2].reshape(PAIR, GROUP_DIMENSION)
        start = jnp.where(own_head, jnp.concatenate([start, start], axis=1), 0.0)
        held[pair] = start.T
    for index, pair in [(i, p) for i in range(tokens // size) for p in range(pairs_here)]:
        rows = (pl.ds(index * size, size), pl.ds(pair * PAIR, PAIR))
        bias, bonus, gain = (ref[:, rows[1]] for ref in (bias_ref, bonus_ref, gain_ref))
        present = row_of + index * size < length
        rec = rec_ref[rows]
        key = jnp.where(present, key_ref[rows], 0.0)
        val = val_ref[rows].astype(BF16)
        total = jnp.where(present, -jnp.exp(bias + decay_ref[rows]), 0.0)
        scores = jnp.where(
            t_of == s_of,
            matmul_nt((rec * bonus).astype(BF16), by_head(key.astype(BF16), first_lanes)),
            0.0,
        )
        before = jnp.zeros_like(total)
        after = jnp.zeros_like(total)
        span = 1
        while span < size:
            later = (row_of & span) != 0
            scaled = (jnp.where(later, rec, key) * jnp.exp(jnp.where(later, before, after))).astype(
                BF16
            )
            pairs = matmul_nt(scaled, by_head(scaled, first_lanes))
            chosen = (
                ((t_of & span) != 0)
                & ((s_of & span) == 0)
                & ((t_of & (-2 * span)) == (s_of & (-2 * span)))
            )
            scores = jnp.where(chosen, pairs, scores)
            partner = jnp.where(
                later, pltpu.roll(total, span, 0), pltpu.roll(total, size - span, 0)
            )
            before = before + jnp.where(later, partner, 0.0)
            after = after + jnp.where(later, 0.0, partner)
            total = total + partner
            span *= 2
        state = held[pair]
        out = matmul(scores.astype(BF16), by_head(val, first_lanes))
        out = out + matmul_nt((rec * jnp.exp(before)).astype(BF16), state.astype(BF16))
        update = matmul_tn(val, (key * jnp.exp(after)).astype(BF16))
        held[pair] = state * jnp.exp(total[:1, :]) + jnp.where(own_head, update, 0.0)
        center = out - split_matmul(out, average)
        spread = split_matmul(center * center, average)
        grouped = center * lax.rsqrt(spread + 0.00064) * gain
        gate = gate_ref[rows]
        gated_ref[rows] = (grouped * (gate / (1.0 + jnp.exp(-gate)))).astype(BF16)
    for pair in range(pairs_here):
        final = held[pair].T
        final = final[:, :GROUP_DIMENSION] + final[:, GROUP_DIMENSION:]
        state_ref[2 * pair : 2 * pair + 2] = final.reshape(2, GROUP_DIMENSION, GROUP_DIMENSION)


def recurrence(length, projected, decay, gate, bias, bonus, gain, start):
    tokens, width = decay.shape
    together = min(2, width // PAIR)
    lanes = together * PAIR
    wide = pl.BlockSpec((tokens, lanes), lambda p: (0, p))
    stacked = [
        pl.BlockSpec((None, tokens, lanes), lambda p, m=m: (m, 0, p)) for m in range(3)
    ]
    row = pl.BlockSpec((1, lanes), lambda p: (0, p))
    states = pl.BlockSpec((2 * together, GROUP_DIMENSION, GROUP_DIMENSION), lambda p: (p, 0, 0))
    return pl.pallas_call(
        recurrence_kernel,
        grid=(width // lanes,),
        in_specs=[pl.BlockSpec(memory_space=pltpu.SMEM)]
        + stacked
        + [wide] * 2
        + [row] * 3
        + [states],
        out_specs=[wide, states],
        out_shape=[
            jax.ShapeDtypeStruct((tokens, width), BF16),
            jax.ShapeDtypeStruct(start.shape, F32),
        ],
        scratch_shapes=[pltpu.VMEM((together, PAIR, PAIR), F32)],
        compiler_params=pltpu.CompilerParams(vmem_limit_bytes=VMEM_BYTES),
        cost_estimate=pl.CostEstimate(
            flops=1 << 20, bytes_accessed=18 * MICROSECOND, transcendentals=0
        ),
        name="recurrence",
    )(length, projected, projected, projected, decay, gate, bias, bonus, gain, start)


def prepare_kernel(
    order_ref,
    length_ref,
    tokens_ref,
    gain_ref,
    first_ref,
    mix_ref,
    stack_ref,
    out3_ref,
    out4_ref,
    last_ref,
    mean_ref,
    root_ref,
):
    step = pl.program_id(0)
    block = out3_ref.shape[1]
    seq_len, width = tokens_ref.shape

    @pl.when(step == 0)
    def _():
        count = min(64, seq_len)
        for index in range(seq_len // count):
            rows = pl.ds(index * count, count)
            values = tokens_ref[rows, :].astype(F32)
            mean = jnp.mean(values, axis=1, keepdims=True)
            center = values - mean
            spread = jnp.mean(center * center, axis=1, keepdims=True)
            mean_ref[rows, :] = jnp.broadcast_to(mean, (count, 128))
            root_ref[rows, :] = jnp.broadcast_to(lax.rsqrt(spread + 1e-05), (count, 128))

    columns = pl.ds(pl.multiple_of(order_ref[step] * block, block), block)
    values = tokens_ref[:, columns].astype(F32)
    normed = (values - mean_ref[:, :1]) * root_ref[:, :1] * gain_ref[:1, columns]
    places = lax.broadcasted_iota(jnp.int32, normed.shape, 0)
    before = jnp.where(places == 0, first_ref[:1, columns], pltpu.roll(normed, 1, 0))
    change = before - normed
    outs = [stack_ref.at[0], stack_ref.at[1], stack_ref.at[2], out3_ref, out4_ref]
    for m, out_ref in enumerate(outs):
        out_ref[...] = (normed + change * mix_ref[m : m + 1, columns]).astype(BF16)
    last = places == length_ref[0] - 1
    last_ref[...] = jnp.sum(jnp.where(last, normed, 0.0), axis=0, keepdims=True)


def prepare(order, length, tokens, gain, first, mixes):
    seq_len, width = tokens.shape
    blocks = order.shape[0]
    block = width // blocks

    def rows(count):
        return pl.BlockSpec((count, width), lambda j, *_: (0, 0))

    moved = pl.BlockSpec((3, seq_len, block), lambda j, *_: (0, 0, j))
    natural = pl.BlockSpec((seq_len, block), lambda j, order, *_: (0, order[j]))
    return pl.pallas_call(
        prepare_kernel,
        grid_spec=pltpu.PrefetchScalarGridSpec(
            num_scalar_prefetch=2,
            grid=(blocks,),
            in_specs=[rows(seq_len), rows(1), rows(1), rows(mixes.shape[0])],
            out_specs=[moved]
            + [natural] * 2
            + [pl.BlockSpec((1, block), lambda j, order, *_: (0, order[j]))],
            scratch_shapes=[pltpu.VMEM((seq_len, 128), F32)] * 2,
        ),
        out_shape=[jax.ShapeDtypeStruct((3, seq_len, width), BF16)]
        + [jax.ShapeDtypeStruct((seq_len, width), BF16)] * 2
        + [jax.ShapeDtypeStruct((1, width), F32)],
        compiler_params=pltpu.CompilerParams(vmem_limit_bytes=VMEM_BYTES),
        cost_estimate=pl.CostEstimate(
            flops=1 << 20, bytes_accessed=22 * MICROSECOND, transcendentals=0
        ),
        name="prepare",
    )(order, length, tokens, gain, first, mixes)


def regroup_kernel(*refs):
    out_ref = refs[-1]
    rows = refs[0].shape[0]
    for at, piece_ref in enumerate(refs[:-1]):
        out_ref[0, at * rows : (at + 1) * rows, :] = piece_ref[...].astype(BF16)


def regroup(pieces, hid):
    rows, width = pieces[0].shape
    wide = width // hid
    tall = rows * len(pieces)
    return pl.pallas_call(
        regroup_kernel,
        grid=(hid,),
        in_specs=[pl.BlockSpec((rows, wide), lambda h: (0, h))] * len(pieces),
        out_specs=pl.BlockSpec((1, tall, wide), lambda h: (h, 0, 0)),
        out_shape=jax.ShapeDtypeStruct((hid, tall, wide), BF16),
        compiler_params=pltpu.CompilerParams(vmem_limit_bytes=VMEM_BYTES),
        cost_estimate=pl.CostEstimate(flops=0, bytes_accessed=20 << 20, transcendentals=0),
        name="regroup",
    )(*pieces)


def project_kernel(*refs):
    values_ref, rows, out_ref = refs[0], refs[1:-1], refs[-1]
    if len(rows[0].shape) == 3:
        total, rows = rows[0][0], rows[1:]
    else:
        total = 0.0
    first = 0
    for rows_ref in rows:
        block = rows_ref[...]
        span = block.shape[0] * block.shape[2]
        values = values_ref[0, :, first : first + span]
        total = total + matmul(values, block.reshape(span, block.shape[3]))
        first += span
    out_ref[0] = total


def project(values, rows, at, of, base=None):
    _, tokens, width = values.shape
    count, wide = rows[0].shape[1], rows[0].shape[3]
    tile = min(256, wide)
    out = pl.BlockSpec((1, tokens, tile), lambda m, n: (m, 0, n))
    return pl.pallas_call(
        project_kernel,
        grid=(count, wide // tile),
        in_specs=[pl.BlockSpec((1, tokens, width // of), lambda m, n: (m, 0, at))]
        + [out] * (base is not None)
        + [
            pl.BlockSpec((r.shape[0], 1, r.shape[2], tile), lambda m, n: (0, m, 0, n))
            for r in rows
        ],
        out_specs=out,
        out_shape=jax.ShapeDtypeStruct((count, tokens, wide), F32),
        compiler_params=pltpu.CompilerParams(vmem_limit_bytes=VMEM_BYTES),
        cost_estimate=pl.CostEstimate(
            flops=2 * count * tokens * width // of * wide,
            bytes_accessed=30 << 20,
            transcendentals=0,
        ),
        name="project",
    )(values, *([] if base is None else [base]), *rows)


def channel_kernel(
    length_ref,
    tokens_ref,
    attended_ref,
    gain_ref,
    first_ref,
    mix_ref,
    middle_ref,
    key_ref,
    accept_ref,
    last_ref,
    held,
):
    step = pl.program_id(0)
    middle = (tokens_ref[...].astype(F32) + attended_ref[...].astype(F32)).astype(BF16)
    middle_ref[...] = middle
    values = middle.astype(F32)
    center = values - jnp.mean(values, axis=1, keepdims=True)
    spread = jnp.mean(center * center, axis=1, keepdims=True)
    normed = center * lax.rsqrt(spread + 1e-05) * gain_ref[...]
    count = normed.shape[0]

    @pl.when(step == 0)
    def _():
        held[...] = first_ref[...]
        last_ref[...] = jnp.zeros_like(last_ref)

    places = lax.broadcasted_iota(jnp.int32, normed.shape, 0)
    before = jnp.where(places == 0, held[...], pltpu.roll(normed, 1, 0))
    held[...] = normed[count - 1 :, :]
    change = before - normed
    key_ref[...] = (normed + change * mix_ref[:1, :]).astype(BF16)
    accept_ref[...] = (normed + change * mix_ref[1:2, :]).astype(BF16)
    last = places + step * count == length_ref[0] - 1
    last_ref[...] += jnp.sum(jnp.where(last, normed, 0.0), axis=0, keepdims=True)


def channel_inputs(length, tokens, attended, gain, first, mixes):
    seq_len, width = tokens.shape
    count = min(64, seq_len)
    tall = pl.BlockSpec((count, width), lambda i: (i, 0))

    def rows(number):
        return pl.BlockSpec((number, width), lambda i: (0, 0))

    return pl.pallas_call(
        channel_kernel,
        grid=(seq_len // count,),
        in_specs=[pl.BlockSpec(memory_space=pltpu.SMEM), tall, tall, rows(1), rows(1), rows(2)],
        out_specs=[tall, tall, tall, rows(1)],
        out_shape=[jax.ShapeDtypeStruct((seq_len, width), BF16)] * 3
        + [jax.ShapeDtypeStruct((1, width), F32)],
        scratch_shapes=[pltpu.VMEM((1, width), F32)],
        compiler_params=pltpu.CompilerParams(vmem_limit_bytes=VMEM_BYTES),
        cost_estimate=pl.CostEstimate(
            flops=1 << 20, bytes_accessed=8 * MICROSECOND, transcendentals=0
        ),
        name="channel_inputs",
    )(length, tokens, attended, gain, first, mixes)


def entry_kernel(places, *refs):
    mixed_ref, rows = refs[0], refs[1 : 1 + len(places)]
    out_ref, held, arrived = refs[1 + len(places) :]
    count, tokens, units = out_ref.shape
    copies = [
        pltpu.make_async_copy(ref, held.at[pl.ds(first, ref.shape[0]), :], arrived.at[at])
        for at, (ref, first) in enumerate(zip(rows, places))
    ]
    for copy in copies:
        copy.start()
    ready = 0
    for at in range(count):
        while ready < len(places) and places[ready] < (at + 1) * units:
            copies[ready].wait()
            ready += 1
        block = held[at * units : (at + 1) * units, :]
        inner = jnp.maximum(matmul_nt(mixed_ref[...], block), 0.0)
        out_ref[at] = (inner * inner).astype(BF16)


def entry_product(mixed, rows, units):
    tokens, width = mixed.shape
    places = [0]
    for block in rows:
        places.append(places[-1] + block.shape[0])
    count = places[-1] // units
    return pl.pallas_call(
        partial(entry_kernel, places[:-1]),
        in_specs=[pl.BlockSpec(memory_space=pltpu.VMEM)]
        + [pl.BlockSpec(memory_space=pl.ANY)] * len(rows),
        out_specs=pl.BlockSpec(memory_space=pltpu.VMEM),
        out_shape=jax.ShapeDtypeStruct((count, tokens, units), BF16),
        scratch_shapes=[
            pltpu.VMEM((places[-1], width), BF16),
            pltpu.SemaphoreType.DMA((len(rows),)),
        ],
        compiler_params=pltpu.CompilerParams(vmem_limit_bytes=VMEM_BYTES),
        cost_estimate=pl.CostEstimate(
            flops=1 << 20, bytes_accessed=15 * MICROSECOND, transcendentals=0
        ),
        name="entry_product",
    )(mixed, *rows)


def exit_kernel(hidden_ref, *refs):
    values, out_ref = refs[:-1], refs[-1]
    units = hidden_ref.shape[2]
    total, at, blocks = 0.0, 0, []
    for values_ref in values:
        blocks.append(values_ref[...])
        if sum(block.shape[0] for block in blocks) == units:
            total = total + matmul(hidden_ref[at], jnp.concatenate(blocks, axis=0))
            at, blocks = at + 1, []
    out_ref[...] = total.astype(BF16)


def exit_product(hidden, values):
    tokens = hidden.shape[1]
    width = values[0].shape[1]
    tile = min(512, width)
    return pl.pallas_call(
        exit_kernel,
        grid=(width // tile,),
        in_specs=[pl.BlockSpec(hidden.shape, lambda n: (0, 0, 0))]
        + [pl.BlockSpec((v.shape[0], tile), lambda n: (0, n)) for v in values],
        out_specs=pl.BlockSpec((tokens, tile), lambda n: (0, n)),
        out_shape=jax.ShapeDtypeStruct((tokens, width), BF16),
        compiler_params=pltpu.CompilerParams(vmem_limit_bytes=VMEM_BYTES),
        cost_estimate=pl.CostEstimate(
            flops=1 << 20, bytes_accessed=7 * MICROSECOND, transcendentals=0
        ),
        name="exit_product",
    )(hidden, *values)


def combine_kernel(slot_ref, length_ref, middle_ref, gate_ref, *refs):
    out_ref = refs[-1]
    present = lax.broadcasted_iota(jnp.int32, gate_ref.shape, 0) < length_ref[0]
    summed = jnp.concatenate([ref[...] for ref in refs[:-1]], axis=1).astype(F32)
    accept = 1.0 / (1.0 + jnp.exp(-gate_ref[...]))
    combined = middle_ref[...].astype(F32) + accept * summed
    out_ref[...] = jnp.where(present, combined, 0.0).astype(BF16)


def combine(slot, length, middle, gate, summed):
    seq_len, wide = gate.shape
    whole = pl.BlockSpec((seq_len, wide), lambda i, *_: (0, 0))
    parts = [pl.BlockSpec(part.shape, lambda i, *_: (0, 0)) for part in summed]
    return pl.pallas_call(
        combine_kernel,
        grid_spec=pltpu.PrefetchScalarGridSpec(
            num_scalar_prefetch=2,
            grid=(1,),
            in_specs=[pl.BlockSpec((seq_len, wide), lambda i, slot, *_: (0, slot[0])), whole]
            + parts,
            out_specs=whole,
        ),
        out_shape=jax.ShapeDtypeStruct((seq_len, wide), BF16),
        compiler_params=pltpu.CompilerParams(vmem_limit_bytes=VMEM_BYTES),
        cost_estimate=pl.CostEstimate(
            flops=1 << 20, bytes_accessed=3 * MICROSECOND, transcendentals=0
        ),
        name="combine",
    )(slot, length, middle, gate, *summed)


def local(
    input_activations,
    prompt_extents,
    continuing_flags,
    owning_index,
    partition_arrangement,
    training_accept_pieces,
    training_lookup_pieces,
    training_content_pieces,
    normalizer_scales,
    prior_step_blends,
    forgetting_bias_vector,
    forgetting_left_lowrank,
    forgetting_right_lowrank,
    instant_emphasis,
    group_normalizer_scale,
    gating_projection,
    mixing_exit_projection,
    kept_summary_places,
    previous_normed_entries,
    feedforward_entry_proj,
    feedforward_exit_proj,
    feedforward_accept_proj,
):
    hid = lax.axis_size("hid")
    req = lax.axis_size("req")
    here = lax.axis_index("req")
    slot = lax.axis_index("hid")
    token_rows = input_activations[0]
    seq_len, width = token_rows.shape
    local_width = mixing_exit_projection.shape[0]
    heads = local_width // GROUP_DIMENSION
    shards = partition_arrangement.shape[0]
    shard_rows = width // shards
    length = prompt_extents[0]
    resuming = continuing_flags[0]

    owned = (resuming == 1) & (owning_index[0] == slot)
    saved = jnp.where(owned, kept_summary_places[0, 0].astype(BF16), 0)
    start = lax.psum_scatter(
        saved.reshape(saved.shape[0], -1), "hid", scatter_dimension=0, tiled=True
    )
    start = start.astype(F32).reshape(heads, GROUP_DIMENSION, GROUP_DIMENSION)

    order = jnp.concatenate(
        [
            lax.dynamic_slice_in_dim(partition_arrangement, (here ^ d) * hid, hid, 0)
            for d in range(req)
        ]
    )
    gain_rows = normalizer_scales.astype(F32)
    mix_rows = prior_step_blends.astype(F32)
    carried = jnp.where(resuming == 1, previous_normed_entries[0].astype(F32), 0.0)
    if shard_rows % 128 == 0:
        blended, decay_in, gate_in, last_in = prepare(
            order, prompt_extents, token_rows, gain_rows[:1], carried[:1], mix_rows[:5]
        )
    else:
        normed_in = layer_norm(token_rows.astype(F32), gain_rows[0])
        before = shifted(normed_in, carried[0])
        rec_in, key_in, val_in, decay_in, gate_in = [
            (normed_in + (before - normed_in) * mix_rows[m][None, :]).astype(BF16)
            for m in range(5)
        ]
        blended = jnp.stack([rec_in, key_in, val_in]).reshape(3, seq_len, shards, shard_rows)
        blended = jnp.take(blended, order, axis=2).reshape(3, seq_len, width)
        last_in = lax.dynamic_slice_in_dim(normed_in, length - 1, 1, 0)

    def side_products(decay_in, gate_in):
        low_rank = jnp.tanh(matmul(decay_in, forgetting_left_lowrank)).astype(BF16)
        return matmul(low_rank, forgetting_right_lowrank), matmul(gate_in, gating_projection)

    def to_heads(columns):
        mine = lax.all_to_all(columns, "hid", split_axis=0, concat_axis=0, tiled=True)
        mine = mine.reshape(hid, -1, shard_rows, local_width)
        return [mine[: hid // 2], mine[hid // 2 :]]

    columns = regroup(
        [training_accept_pieces, training_lookup_pieces, training_content_pieces], hid
    )
    units = feedforward_entry_proj.shape[0]
    hold = lax.optimization_barrier
    if req == 4:
        half = units // 2
        cut = half * 5 // 7 // 16 * 16
        key_mine, value_mine = feedforward_entry_proj, feedforward_exit_proj
        key_x, key_y = across(key_mine, 1), across(key_mine, 2)
        mine = to_heads(columns)
        decay, gate = side_products(decay_in, gate_in)
        mine, key_x, key_y, blended, decay, gate, start = hold(
            (mine, key_x, key_y, blended, decay, gate, start)
        )
        trained = [mine, [across(rows, 1) for rows in mine], [across(rows, 2) for rows in mine]]
        first = [key_x[:cut], key_y[half : half + cut]]
        second = [key_x[cut:half], key_y[half + cut :]]
        trained, first, second = hold((trained, first, second))
        opposite = [across(trained[1][0], 2), across(trained[2][1], 1)]
        projected = project(blended, sum(trained, []), 0, 1)
        projected, opposite, first = hold((projected, opposite, first))
        key_far = [across(first[0], 2), across(first[1], 1)]
        projected = project(blended, opposite, 3, 4, projected)
    else:
        decay, gate = side_products(decay_in, gate_in)
        low, high = [whole(side, req) for side in to_heads(columns)]
        projected = project(blended, [side[d] for d in range(req) for side in (low, high)], 0, 1)
    gated, new_state = recurrence(
        prompt_extents,
        projected,
        decay,
        gate,
        forgetting_bias_vector[None],
        instant_emphasis[None],
        group_normalizer_scale[None],
        start,
    )
    if req == 4:
        gated, value_mine, second, key_far = hold((gated, value_mine, second, key_far))
    head_terms = matmul(gated, mixing_exit_projection).astype(BF16)
    attended = lax.psum(head_terms, "hid")
    if req == 4:
        value_x, value_y = across(value_mine, 1), across(value_mine, 2)
        key_far.insert(1, across(second[0], 2))
        key_far.append(across(second[1], 1))
        value_far = [value_x[:half], value_y[half:]]
        attended, key_far, value_far = hold((attended, key_far, value_far))
        value_far = [across(value_far[0], 2), across(value_far[1], 1)]
        key_rows = [key_mine, key_x, key_y, *key_far]
        value_rows = [value_mine, value_x, value_y, *value_far]
    else:
        key_rows = whole(feedforward_entry_proj, req)
        value_rows = whole(feedforward_exit_proj, req)
    middle, mixed_key, mixed_accept, last_chan = channel_inputs(
        prompt_extents, token_rows, attended, gain_rows[1:], carried[1:], mix_rows[5:]
    )
    accept = matmul(mixed_accept, feedforward_accept_proj)
    hidden = entry_product(mixed_key, key_rows, units)
    terms = exit_product(hidden, value_rows)
    summed = lax.psum_scatter(terms, "hid", scatter_dimension=1, tiled=True)
    layer_out = combine(slot[None], prompt_extents, middle, accept, [summed])[None]
    shift_out = jnp.concatenate([last_in, last_chan]).astype(BF16)[None]
    return (layer_out, new_state[None], shift_out)


def solution(mesh):
    placed = (
        P("req", None, None),
        P("req"),
        P("req"),
        P("req"),
        P(),
        P(("req", "hid"), None),
        P(("req", "hid"), None),
        P(("req", "hid"), None),
        P(),
        P(),
        P("hid"),
        P(),
        P(None, "hid"),
        P("hid"),
        P("hid"),
        P(None, "hid"),
        P("hid", None),
        P("req", "hid", None, None, None),
        P("req", None, None),
        P(("req", "hid"), None),
        P(("req", "hid"), None),
        P(None, "hid"),
    )
    return jax.shard_map(
        local,
        mesh=mesh,
        in_specs=placed,
        out_specs=(P("req", None, "hid"), P("req", "hid", None, None), P("req", None, None)),
        check_vma=False,
    )
```

```python
from functools import partial

import jax
import jax.numpy as jnp
from jax import lax
from jax.experimental import pallas as pl
from jax.experimental.pallas import tpu as pltpu
from jax.sharding import PartitionSpec as P

GROUP_DIMENSION = 64
PAIR = 2 * GROUP_DIMENSION
CHUNK = 64
BF16 = jnp.bfloat16
F32 = jnp.float32
MICROSECOND = 3690000
VMEM_BYTES = 60 << 20


def layer_norm(values, gain):
    center = values - jnp.mean(values, axis=-1, keepdims=True)
    spread = jnp.mean(center * center, axis=-1, keepdims=True)
    return center / jnp.sqrt(spread + 1e-05) * gain


def shifted(values, first_row):
    return jnp.concatenate([first_row[None, :], values[:-1]], axis=0)


def matmul(a, b):
    return jnp.dot(a, b, preferred_element_type=F32)


def matmul_nt(a, b):
    return lax.dot_general(a, b, (((1,), (1,)), ((), ())), preferred_element_type=F32)


def matmul_tn(a, b):
    return lax.dot_general(a, b, (((0,), (0,)), ((), ())), preferred_element_type=F32)


def across(value, axis):
    return lax.ppermute(value, "req", [(i, i ^ axis) for i in range(4)])


def whole(value, req):
    blocks = lax.all_gather(value, "req", axis=0, tiled=False)
    me = lax.axis_index("req")
    return [lax.dynamic_index_in_dim(blocks, me ^ d, 0, keepdims=False) for d in range(req)]


def by_head(values, first_lanes):
    zeros = jnp.zeros_like(values)
    return jnp.concatenate(
        [jnp.where(first_lanes, values, zeros), jnp.where(first_lanes, zeros, values)], axis=0
    )


def split_matmul(values, weights):
    high = values.astype(BF16)
    low = (values - high.astype(F32)).astype(BF16)
    return matmul(high, weights) + matmul(low, weights)


def recurrence_kernel(
    steps,
    count,
    length_ref,
    base_ref,
    values_ref,
    *refs,
):
    rows_far, refs = refs[:count], refs[count:]
    decay_ref, gate_ref, bias_ref, bonus_ref, gain_ref, start_ref, exit_ref = refs[:7]
    terms_ref, state_ref, held, projected, gated_ref, total_ref = refs[7:]
    rec_ref, key_ref, val_ref = (projected.at[m] for m in range(3))
    for m in range(3):
        projected[m] = rows_product(base_ref[m], values_ref, m, rows_far)
    length = length_ref[0]
    tokens = base_ref.shape[1]
    size = min(CHUNK, tokens)
    lanes = lax.broadcasted_iota(jnp.int32, (size, PAIR), 1)
    first_lanes = lanes < GROUP_DIMENSION
    row_of = lax.broadcasted_iota(jnp.int32, (size, PAIR), 0)
    t_of = lax.broadcasted_iota(jnp.int32, (size, 2 * size), 0)
    s_of = lax.broadcasted_iota(jnp.int32, (size, 2 * size), 1) & (size - 1)
    side_a = lax.broadcasted_iota(jnp.int32, (PAIR, PAIR), 0) < GROUP_DIMENSION
    side_b = lax.broadcasted_iota(jnp.int32, (PAIR, PAIR), 1) < GROUP_DIMENSION
    own_head = side_a == side_b
    average = jnp.where(own_head, 1.0 / GROUP_DIMENSION, 0.0).astype(BF16)
    pairs_here = base_ref.shape[2] // PAIR
    for pair in range(pairs_here):
        start = start_ref[2 * pair : 2 * pair + 2].reshape(PAIR, GROUP_DIMENSION)
        start = jnp.where(own_head, jnp.concatenate([start, start], axis=1), 0.0)
        held[pair] = start.T
    for index, pair in [(i, p) for i in range(tokens // size) for p in range(pairs_here)]:
        rows = (pl.ds(index * size, size), pl.ds(pair * PAIR, PAIR))
        bias, bonus, gain = (ref[:, rows[1]] for ref in (bias_ref, bonus_ref, gain_ref))
        present = row_of + index * size < length
        rec = rec_ref[rows]
        key = jnp.where(present, key_ref[rows], 0.0)
        val = val_ref[rows].astype(BF16)
        total = jnp.where(present, -jnp.exp(bias + decay_ref[rows]), 0.0)
        scores = jnp.where(
            t_of == s_of,
            matmul_nt((rec * bonus).astype(BF16), by_head(key.astype(BF16), first_lanes)),
            0.0,
        )
        before = jnp.zeros_like(total)
        after = jnp.zeros_like(total)
        span = 1
        while span < size:
            later = (row_of & span) != 0
            scaled = (jnp.where(later, rec, key) * jnp.exp(jnp.where(later, before, after))).astype(
                BF16
            )
            pairs = matmul_nt(scaled, by_head(scaled, first_lanes))
            chosen = (
                ((t_of & span) != 0)
                & ((s_of & span) == 0)
                & ((t_of & (-2 * span)) == (s_of & (-2 * span)))
            )
            scores = jnp.where(chosen, pairs, scores)
            partner = jnp.where(
                later, pltpu.roll(total, span, 0), pltpu.roll(total, size - span, 0)
            )
            before = before + jnp.where(later, partner, 0.0)
            after = after + jnp.where(later, 0.0, partner)
            total = total + partner
            span *= 2
        state = held[pair]
        out = matmul(scores.astype(BF16), by_head(val, first_lanes))
        out = out + matmul_nt((rec * jnp.exp(before)).astype(BF16), state.astype(BF16))
        update = matmul_tn(val, (key * jnp.exp(after)).astype(BF16))
        held[pair] = state * jnp.exp(total[:1, :]) + jnp.where(own_head, update, 0.0)
        center = out - split_matmul(out, average)
        spread = split_matmul(center * center, average)
        grouped = center * lax.rsqrt(spread + 0.00064) * gain
        gate = gate_ref[rows]
        gated_ref[rows] = (grouped * (gate / (1.0 + jnp.exp(-gate)))).astype(BF16)
    for pair in range(pairs_here):
        final = held[pair].T
        final = final[:, :GROUP_DIMENSION] + final[:, GROUP_DIMENSION:]
        state_ref[2 * pair : 2 * pair + 2] = final.reshape(2, GROUP_DIMENSION, GROUP_DIMENSION)
    step = pl.program_id(0)
    width = exit_ref.shape[1]
    tile = min(1024, width)
    for first in range(0, width, tile):
        columns = slice(first, first + tile)
        part = matmul(gated_ref[...], exit_ref[:, columns])
        if steps == 1:
            terms_ref[:, columns] = part.astype(BF16)
            continue

        @pl.when(step == 0)
        def _():
            total_ref[:, columns] = part

        @pl.when((step > 0) & (step < steps - 1))
        def _():
            total_ref[:, columns] += part

        @pl.when(step == steps - 1)
        def _():
            terms_ref[:, columns] = (total_ref[:, columns] + part).astype(BF16)


def recurrence(length, base, values, far, decay, gate, bias, bonus, gain, start, exit_rows):
    tokens, width = decay.shape
    out_width = exit_rows.shape[1]
    together = min(2, width // PAIR)
    lanes = together * PAIR
    steps = width // lanes
    reach = sum(r.shape[0] * r.shape[2] for r in far) or 128
    place = values.shape[2] // reach - 1
    wide = pl.BlockSpec((tokens, lanes), lambda p: (0, p))
    row = pl.BlockSpec((1, lanes), lambda p: (0, p))
    states = pl.BlockSpec((2 * together, GROUP_DIMENSION, GROUP_DIMENSION), lambda p: (p, 0, 0))
    return pl.pallas_call(
        partial(recurrence_kernel, steps, len(far)),
        grid=(steps,),
        in_specs=[
            pl.BlockSpec(memory_space=pltpu.SMEM),
            pl.BlockSpec((3, tokens, lanes), lambda p: (0, 0, p)),
            pl.BlockSpec((3, tokens, reach), lambda p: (0, 0, place)),
        ]
        + [pl.BlockSpec((*r.shape[:3], lanes), lambda p: (0, 0, 0, p)) for r in far]
        + [wide] * 2
        + [row] * 3
        + [states, pl.BlockSpec((lanes, out_width), lambda p: (p, 0))],
        out_specs=[pl.BlockSpec((tokens, out_width), lambda p: (0, 0)), states],
        out_shape=[
            jax.ShapeDtypeStruct((tokens, out_width), BF16),
            jax.ShapeDtypeStruct(start.shape, F32),
        ],
        scratch_shapes=[
            pltpu.VMEM((together, PAIR, PAIR), F32),
            pltpu.VMEM((3, tokens, lanes), F32),
            pltpu.VMEM((tokens, lanes), BF16),
            pltpu.VMEM((tokens, out_width), F32),
        ],
        compiler_params=pltpu.CompilerParams(vmem_limit_bytes=VMEM_BYTES),
        cost_estimate=pl.CostEstimate(
            flops=1 << 20, bytes_accessed=24 * MICROSECOND, transcendentals=0
        ),
        name="recurrence",
    )(length, base, values, *far, decay, gate, bias, bonus, gain, start, exit_rows)


def prepare_kernel(
    order_ref,
    length_ref,
    tokens_ref,
    gain_ref,
    first_ref,
    mix_ref,
    stack_ref,
    out3_ref,
    out4_ref,
    last_ref,
    mean_ref,
    root_ref,
):
    step = pl.program_id(0)
    block = out3_ref.shape[1]
    seq_len, width = tokens_ref.shape

    @pl.when(step == 0)
    def _():
        count = min(64, seq_len)
        for index in range(seq_len // count):
            rows = pl.ds(index * count, count)
            values = tokens_ref[rows, :].astype(F32)
            mean = jnp.mean(values, axis=1, keepdims=True)
            center = values - mean
            spread = jnp.mean(center * center, axis=1, keepdims=True)
            mean_ref[rows, :] = jnp.broadcast_to(mean, (count, 128))
            root_ref[rows, :] = jnp.broadcast_to(lax.rsqrt(spread + 1e-05), (count, 128))

    columns = pl.ds(pl.multiple_of(order_ref[step] * block, block), block)
    values = tokens_ref[:, columns].astype(F32)
    normed = (values - mean_ref[:, :1]) * root_ref[:, :1] * gain_ref[:1, columns]
    places = lax.broadcasted_iota(jnp.int32, normed.shape, 0)
    before = jnp.where(places == 0, first_ref[:1, columns], pltpu.roll(normed, 1, 0))
    change = before - normed
    outs = [stack_ref.at[0], stack_ref.at[1], stack_ref.at[2], out3_ref, out4_ref]
    for m, out_ref in enumerate(outs):
        out_ref[...] = (normed + change * mix_ref[m : m + 1, columns]).astype(BF16)
    last = places == length_ref[0] - 1
    last_ref[...] = jnp.sum(jnp.where(last, normed, 0.0), axis=0, keepdims=True)


def prepare(order, length, tokens, gain, first, mixes):
    seq_len, width = tokens.shape
    blocks = order.shape[0]
    block = width // blocks

    def rows(count):
        return pl.BlockSpec((count, width), lambda j, *_: (0, 0))

    moved = pl.BlockSpec((3, seq_len, block), lambda j, *_: (0, 0, j))
    natural = pl.BlockSpec((seq_len, block), lambda j, order, *_: (0, order[j]))
    return pl.pallas_call(
        prepare_kernel,
        grid_spec=pltpu.PrefetchScalarGridSpec(
            num_scalar_prefetch=2,
            grid=(blocks,),
            in_specs=[rows(seq_len), rows(1), rows(1), rows(mixes.shape[0])],
            out_specs=[moved]
            + [natural] * 2
            + [pl.BlockSpec((1, block), lambda j, order, *_: (0, order[j]))],
            scratch_shapes=[pltpu.VMEM((seq_len, 128), F32)] * 2,
        ),
        out_shape=[jax.ShapeDtypeStruct((3, seq_len, width), BF16)]
        + [jax.ShapeDtypeStruct((seq_len, width), BF16)] * 2
        + [jax.ShapeDtypeStruct((1, width), F32)],
        compiler_params=pltpu.CompilerParams(vmem_limit_bytes=VMEM_BYTES),
        cost_estimate=pl.CostEstimate(
            flops=1 << 20, bytes_accessed=22 * MICROSECOND, transcendentals=0
        ),
        name="prepare",
    )(order, length, tokens, gain, first, mixes)


def regroup_kernel(*refs):
    out_ref = refs[-1]
    rows = refs[0].shape[0]
    for at, piece_ref in enumerate(refs[:-1]):
        out_ref[0, at * rows : (at + 1) * rows, :] = piece_ref[...].astype(BF16)


def regroup(pieces, hid):
    rows, width = pieces[0].shape
    wide = width // hid
    tall = rows * len(pieces)
    return pl.pallas_call(
        regroup_kernel,
        grid=(hid,),
        in_specs=[pl.BlockSpec((rows, wide), lambda h: (0, h))] * len(pieces),
        out_specs=pl.BlockSpec((1, tall, wide), lambda h: (h, 0, 0)),
        out_shape=jax.ShapeDtypeStruct((hid, tall, wide), BF16),
        compiler_params=pltpu.CompilerParams(vmem_limit_bytes=VMEM_BYTES),
        cost_estimate=pl.CostEstimate(flops=0, bytes_accessed=20 << 20, transcendentals=0),
        name="regroup",
    )(*pieces)


def rows_product(total, values_ref, m, rows):
    first = 0
    for rows_ref in rows:
        block = rows_ref[:, m]
        span = block.shape[0] * block.shape[1]
        values = values_ref[m, :, first : first + span]
        total = total + matmul(values, block.reshape(span, block.shape[2]))
        first += span
    return total


def project_kernel(values_ref, *refs):
    refs[-1][0] = rows_product(0.0, values_ref, 0, refs[:-1])


def project(values, rows):
    count, tokens, width = values.shape
    wide = rows[0].shape[-1]
    tile = min(256, wide)
    out = pl.BlockSpec((1, tokens, tile), lambda m, n: (m, 0, n))
    return pl.pallas_call(
        project_kernel,
        grid=(count, wide // tile),
        in_specs=[pl.BlockSpec((1, tokens, width), lambda m, n: (m, 0, 0))]
        + [
            pl.BlockSpec((r.shape[0], 1, r.shape[2], tile), lambda m, n: (0, m, 0, n))
            for r in rows
        ],
        out_specs=out,
        out_shape=jax.ShapeDtypeStruct((count, tokens, wide), F32),
        compiler_params=pltpu.CompilerParams(vmem_limit_bytes=VMEM_BYTES),
        cost_estimate=pl.CostEstimate(
            flops=1 << 20, bytes_accessed=13 * MICROSECOND, transcendentals=0
        ),
        name="project",
    )(values, *rows)


def channel_kernel(places, steps, length_ref, tokens_ref, attended_ref, gain_ref, first_ref, mix_ref, *refs):
    count = len(places)
    rows, refs = refs[:count], refs[count:]
    hidden_ref, accept_ref, last_ref, held, mixed, taken, arrived = refs
    step = pl.program_id(0)
    copies = [
        pltpu.make_async_copy(ref, taken.at[pl.ds(first, ref.shape[0]), :], arrived.at[at])
        for at, (ref, first) in enumerate(zip(rows, places))
    ]

    @pl.when(step == 0)
    def _():
        for copy in copies:
            copy.start()
        held[...] = first_ref[...]
        last_ref[...] = jnp.zeros_like(last_ref)

    middle = (tokens_ref[...].astype(F32) + attended_ref[...].astype(F32)).astype(BF16)
    values = middle.astype(F32)
    center = values - jnp.mean(values, axis=1, keepdims=True)
    spread = jnp.mean(center * center, axis=1, keepdims=True)
    normed = center * lax.rsqrt(spread + 1e-05) * gain_ref[...]
    tall = normed.shape[0]
    row_of = lax.broadcasted_iota(jnp.int32, normed.shape, 0)
    before = jnp.where(row_of == 0, held[...], pltpu.roll(normed, 1, 0))
    held[...] = normed[tall - 1 :, :]
    change = before - normed
    mixed[pl.ds(pl.multiple_of(step * tall, tall), tall), :] = (
        normed + change * mix_ref[:1, :]
    ).astype(BF16)
    accept_ref[...] = (normed + change * mix_ref[1:2, :]).astype(BF16)
    place = length_ref[0] - 1 - step * tall

    @pl.when((place >= 0) & (place < tall))
    def _():
        last_ref[...] = jnp.sum(jnp.where(row_of == place, normed, 0.0), axis=0, keepdims=True)

    @pl.when(step == steps - 1)
    def _():
        blocks, _, units = hidden_ref.shape
        ready = 0
        for at in range(blocks):
            while ready < count and places[ready] < (at + 1) * units:
                copies[ready].wait()
                ready += 1
            inner = matmul_nt(mixed[...], taken[at * units : (at + 1) * units, :])
            inner = jnp.maximum(inner, 0.0)
            hidden_ref[at] = (inner * inner).astype(BF16)


def channel_inputs(length, tokens, attended, gain, first, mixes, rows, units):
    seq_len, width = tokens.shape
    tall = min(64, seq_len)
    steps = seq_len // tall
    by_rows = pl.BlockSpec((tall, width), lambda i: (i, 0))
    places = [0]
    for block in rows:
        places.append(places[-1] + block.shape[0])
    blocks = places[-1] // units

    def wide(number):
        return pl.BlockSpec((number, width), lambda i: (0, 0))

    return pl.pallas_call(
        partial(channel_kernel, places[:-1], steps),
        grid=(steps,),
        in_specs=[
            pl.BlockSpec(memory_space=pltpu.SMEM),
            by_rows,
            by_rows,
            wide(1),
            wide(1),
            wide(2),
        ]
        + [pl.BlockSpec(memory_space=pl.ANY)] * len(rows),
        out_specs=[
            pl.BlockSpec((blocks, seq_len, units), lambda i: (0, 0, 0)),
            by_rows,
            wide(1),
        ],
        out_shape=[
            jax.ShapeDtypeStruct((blocks, seq_len, units), BF16),
            jax.ShapeDtypeStruct((seq_len, width), BF16),
            jax.ShapeDtypeStruct((1, width), F32),
        ],
        scratch_shapes=[
            pltpu.VMEM((1, width), F32),
            pltpu.VMEM((seq_len, width), BF16),
            pltpu.VMEM((places[-1], width), BF16),
            pltpu.SemaphoreType.DMA((len(rows),)),
        ],
        compiler_params=pltpu.CompilerParams(vmem_limit_bytes=VMEM_BYTES),
        cost_estimate=pl.CostEstimate(
            flops=1 << 20, bytes_accessed=22 * MICROSECOND, transcendentals=0
        ),
        name="channel_inputs",
    )(length, tokens, attended, gain, first, mixes, *rows)


def exit_kernel(hidden_ref, *refs):
    values, out_ref = refs[:-1], refs[-1]
    units = hidden_ref.shape[2]
    total, at, blocks = 0.0, 0, []
    for values_ref in values:
        blocks.append(values_ref[...])
        if sum(block.shape[0] for block in blocks) == units:
            total = total + matmul(hidden_ref[at], jnp.concatenate(blocks, axis=0))
            at, blocks = at + 1, []
    out_ref[...] = total.astype(BF16)


def exit_product(hidden, values):
    tokens = hidden.shape[1]
    width = values[0].shape[1]
    tile = min(512, width)
    return pl.pallas_call(
        exit_kernel,
        grid=(width // tile,),
        in_specs=[pl.BlockSpec(hidden.shape, lambda n: (0, 0, 0))]
        + [pl.BlockSpec((v.shape[0], tile), lambda n: (0, n)) for v in values],
        out_specs=pl.BlockSpec((tokens, tile), lambda n: (0, n)),
        out_shape=jax.ShapeDtypeStruct((tokens, width), BF16),
        compiler_params=pltpu.CompilerParams(vmem_limit_bytes=VMEM_BYTES),
        cost_estimate=pl.CostEstimate(
            flops=1 << 20, bytes_accessed=7 * MICROSECOND, transcendentals=0
        ),
        name="exit_product",
    )(hidden, *values)


def combine_kernel(slot_ref, length_ref, tokens_ref, attended_ref, gate_ref, *refs):
    out_ref = refs[-1]
    present = lax.broadcasted_iota(jnp.int32, gate_ref.shape, 0) < length_ref[0]
    summed = jnp.concatenate([ref[...] for ref in refs[:-1]], axis=1).astype(F32)
    accept = 1.0 / (1.0 + jnp.exp(-gate_ref[...]))
    middle = (tokens_ref[...].astype(F32) + attended_ref[...].astype(F32)).astype(BF16)
    combined = middle.astype(F32) + accept * summed
    out_ref[...] = jnp.where(present, combined, 0.0).astype(BF16)


def combine(slot, length, tokens, attended, gate, summed):
    seq_len, wide = gate.shape
    whole = pl.BlockSpec((seq_len, wide), lambda i, *_: (0, 0))
    parts = [pl.BlockSpec(part.shape, lambda i, *_: (0, 0)) for part in summed]
    return pl.pallas_call(
        combine_kernel,
        grid_spec=pltpu.PrefetchScalarGridSpec(
            num_scalar_prefetch=2,
            grid=(1,),
            in_specs=[pl.BlockSpec((seq_len, wide), lambda i, slot, *_: (0, slot[0]))] * 2
            + [whole]
            + parts,
            out_specs=whole,
        ),
        out_shape=jax.ShapeDtypeStruct((seq_len, wide), BF16),
        compiler_params=pltpu.CompilerParams(vmem_limit_bytes=VMEM_BYTES),
        cost_estimate=pl.CostEstimate(
            flops=1 << 20, bytes_accessed=3 * MICROSECOND, transcendentals=0
        ),
        name="combine",
    )(slot, length, tokens, attended, gate, *summed)


def local(
    input_activations,
    prompt_extents,
    continuing_flags,
    owning_index,
    partition_arrangement,
    training_accept_pieces,
    training_lookup_pieces,
    training_content_pieces,
    normalizer_scales,
    prior_step_blends,
    forgetting_bias_vector,
    forgetting_left_lowrank,
    forgetting_right_lowrank,
    instant_emphasis,
    group_normalizer_scale,
    gating_projection,
    mixing_exit_projection,
    kept_summary_places,
    previous_normed_entries,
    feedforward_entry_proj,
    feedforward_exit_proj,
    feedforward_accept_proj,
):
    hid = lax.axis_size("hid")
    req = lax.axis_size("req")
    here = lax.axis_index("req")
    slot = lax.axis_index("hid")
    token_rows = input_activations[0]
    seq_len, width = token_rows.shape
    local_width = mixing_exit_projection.shape[0]
    heads = local_width // GROUP_DIMENSION
    shards = partition_arrangement.shape[0]
    shard_rows = width // shards
    length = prompt_extents[0]
    resuming = continuing_flags[0]

    owned = (resuming == 1) & (owning_index[0] == slot)
    saved = jnp.where(owned, kept_summary_places[0, 0].astype(BF16), 0)
    start = lax.psum_scatter(
        saved.reshape(saved.shape[0], -1), "hid", scatter_dimension=0, tiled=True
    )
    start = start.astype(F32).reshape(heads, GROUP_DIMENSION, GROUP_DIMENSION)

    order = jnp.concatenate(
        [
            lax.dynamic_slice_in_dim(partition_arrangement, (here ^ d) * hid, hid, 0)
            for d in range(req)
        ]
    )
    gain_rows = normalizer_scales.astype(F32)
    mix_rows = prior_step_blends.astype(F32)
    carried = jnp.where(resuming == 1, previous_normed_entries[0].astype(F32), 0.0)
    if shard_rows % 128 == 0:
        blended, decay_in, gate_in, last_in = prepare(
            order, prompt_extents, token_rows, gain_rows[:1], carried[:1], mix_rows[:5]
        )
    else:
        normed_in = layer_norm(token_rows.astype(F32), gain_rows[0])
        before = shifted(normed_in, carried[0])
        rec_in, key_in, val_in, decay_in, gate_in = [
            (normed_in + (before - normed_in) * mix_rows[m][None, :]).astype(BF16)
            for m in range(5)
        ]
        blended = jnp.stack([rec_in, key_in, val_in]).reshape(3, seq_len, shards, shard_rows)
        blended = jnp.take(blended, order, axis=2).reshape(3, seq_len, width)
        last_in = lax.dynamic_slice_in_dim(normed_in, length - 1, 1, 0)

    def side_products(decay_in, gate_in):
        low_rank = jnp.tanh(matmul(decay_in, forgetting_left_lowrank)).astype(BF16)
        return matmul(low_rank, forgetting_right_lowrank), matmul(gate_in, gating_projection)

    def to_heads(columns):
        mine = lax.all_to_all(columns, "hid", split_axis=0, concat_axis=0, tiled=True)
        mine = mine.reshape(hid, -1, shard_rows, local_width)
        return [mine[: hid // 2], mine[hid // 2 :]]

    columns = regroup(
        [training_accept_pieces, training_lookup_pieces, training_content_pieces], hid
    )
    units = feedforward_entry_proj.shape[0]
    hold = lax.optimization_barrier
    if req == 4:
        half = units // 2
        cut = half * 5 // 7 // 16 * 16
        key_mine, value_mine = feedforward_entry_proj, feedforward_exit_proj
        key_x, key_y = across(key_mine, 1), across(key_mine, 2)
        mine = to_heads(columns)
        decay, gate = side_products(decay_in, gate_in)
        mine, key_x, key_y, blended, decay, gate, start = hold(
            (mine, key_x, key_y, blended, decay, gate, start)
        )
        trained = [mine, [across(rows, 1) for rows in mine], [across(rows, 2) for rows in mine]]
        first = [key_x[:cut], key_y[half : half + cut]]
        second = [key_x[cut:half], key_y[half + cut :]]
        trained, first, second = hold((trained, first, second))
        opposite = [across(trained[1][0], 2), across(trained[2][1], 1)]
        projected = project(blended, sum(trained, []))
        projected, opposite, first = hold((projected, opposite, first))
        key_far = [across(first[0], 2), across(first[1], 1)]
    else:
        decay, gate = side_products(decay_in, gate_in)
        low, high = [whole(side, req) for side in to_heads(columns)]
        opposite = []
        projected = project(blended, [side[d] for d in range(req) for side in (low, high)])
    head_terms, new_state = recurrence(
        prompt_extents,
        projected,
        blended,
        opposite,
        decay,
        gate,
        forgetting_bias_vector[None],
        instant_emphasis[None],
        group_normalizer_scale[None],
        start,
        mixing_exit_projection,
    )
    if req == 4:
        head_terms, value_mine, second, key_far = hold(
            (head_terms, value_mine, second, key_far)
        )
    attended = lax.psum(head_terms, "hid")
    if req == 4:
        value_x, value_y = across(value_mine, 1), across(value_mine, 2)
        key_far.insert(1, across(second[0], 2))
        key_far.append(across(second[1], 1))
        value_far = [value_x[:half], value_y[half:]]
        value_far, key_far = hold((value_far, key_far))
        value_far = [across(value_far[0], 2), across(value_far[1], 1)]
        key_rows = [key_mine, key_x, key_y, *key_far]
        value_rows = [value_mine, value_x, value_y, *value_far]
    else:
        key_rows = whole(feedforward_entry_proj, req)
        value_rows = whole(feedforward_exit_proj, req)
    hidden, accept_in, last_chan = channel_inputs(
        prompt_extents,
        token_rows,
        attended,
        gain_rows[1:],
        carried[1:],
        mix_rows[5:],
        key_rows,
        units,
    )
    accept = matmul(accept_in, feedforward_accept_proj)
    terms = exit_product(hidden, value_rows)
    summed = lax.psum_scatter(terms, "hid", scatter_dimension=1, tiled=True)
    layer_out = combine(
        slot[None], prompt_extents, token_rows, attended, accept, [summed]
    )[None]
    shift_out = jnp.concatenate([last_in, last_chan]).astype(BF16)[None]
    return (layer_out, new_state[None], shift_out)


def solution(mesh):
    placed = (
        P("req", None, None),
        P("req"),
        P("req"),
        P("req"),
        P(),
        P(("req", "hid"), None),
        P(("req", "hid"), None),
        P(("req", "hid"), None),
        P(),
        P(),
        P("hid"),
        P(),
        P(None, "hid"),
        P("hid"),
        P("hid"),
        P(None, "hid"),
        P("hid", None),
        P("req", "hid", None, None, None),
        P("req", None, None),
        P(("req", "hid"), None),
        P(("req", "hid"), None),
        P(None, "hid"),
    )
    return jax.shard_map(
        local,
        mesh=mesh,
        in_specs=placed,
        out_specs=(P("req", None, "hid"), P("req", "hid", None, None), P("req", None, None)),
        check_vma=False,
    )
```

```python
from functools import partial

import jax
import jax.numpy as jnp
from jax import lax
from jax.experimental import pallas as pl
from jax.experimental.pallas import tpu as pltpu
from jax.sharding import PartitionSpec as P

GROUP_DIMENSION = 64
PAIR = 2 * GROUP_DIMENSION
CHUNK = 64
BF16 = jnp.bfloat16
F32 = jnp.float32
MICROSECOND = 3690000
VMEM_BYTES = 60 << 20


def layer_norm(values, gain):
    center = values - jnp.mean(values, axis=-1, keepdims=True)
    spread = jnp.mean(center * center, axis=-1, keepdims=True)
    return center / jnp.sqrt(spread + 1e-05) * gain


def shifted(values, first_row):
    return jnp.concatenate([first_row[None, :], values[:-1]], axis=0)


def matmul(a, b):
    return jnp.dot(a, b, preferred_element_type=F32)


def matmul_nt(a, b):
    return lax.dot_general(a, b, (((1,), (1,)), ((), ())), preferred_element_type=F32)


def matmul_tn(a, b):
    return lax.dot_general(a, b, (((0,), (0,)), ((), ())), preferred_element_type=F32)


def across(value, axis):
    return lax.ppermute(value, "req", [(i, i ^ axis) for i in range(4)])


def whole(value, req):
    blocks = lax.all_gather(value, "req", axis=0, tiled=False)
    me = lax.axis_index("req")
    return [lax.dynamic_index_in_dim(blocks, me ^ d, 0, keepdims=False) for d in range(req)]


def by_head(values, first_lanes):
    zeros = jnp.zeros_like(values)
    return jnp.concatenate(
        [jnp.where(first_lanes, values, zeros), jnp.where(first_lanes, zeros, values)], axis=0
    )


def split_matmul(values, weights):
    high = values.astype(BF16)
    low = (values - high.astype(F32)).astype(BF16)
    return matmul(high, weights) + matmul(low, weights)


def recurrence_kernel(
    steps,
    count,
    length_ref,
    base_ref,
    values_ref,
    *refs,
):
    rows_far, refs = refs[:count], refs[count:]
    decay_ref, gate_ref, bias_ref, bonus_ref, gain_ref, start_ref, exit_ref = refs[:7]
    terms_ref, state_ref, held, projected, gated_ref, total_ref = refs[7:]
    rec_ref, key_ref, val_ref = (projected.at[m] for m in range(3))
    for m in range(3):
        projected[m] = rows_product(base_ref[m], values_ref, m, rows_far)
    length = length_ref[0]
    tokens = base_ref.shape[1]
    size = min(CHUNK, tokens)
    lanes = lax.broadcasted_iota(jnp.int32, (size, PAIR), 1)
    first_lanes = lanes < GROUP_DIMENSION
    row_of = lax.broadcasted_iota(jnp.int32, (size, PAIR), 0)
    t_of = lax.broadcasted_iota(jnp.int32, (size, 2 * size), 0)
    s_of = lax.broadcasted_iota(jnp.int32, (size, 2 * size), 1) & (size - 1)
    side_a = lax.broadcasted_iota(jnp.int32, (PAIR, PAIR), 0) < GROUP_DIMENSION
    side_b = lax.broadcasted_iota(jnp.int32, (PAIR, PAIR), 1) < GROUP_DIMENSION
    own_head = side_a == side_b
    average = jnp.where(own_head, 1.0 / GROUP_DIMENSION, 0.0).astype(BF16)
    pairs_here = base_ref.shape[2] // PAIR
    for pair in range(pairs_here):
        start = start_ref[2 * pair : 2 * pair + 2].reshape(PAIR, GROUP_DIMENSION)
        start = jnp.where(own_head, jnp.concatenate([start, start], axis=1), 0.0)
        held[pair] = start.T
    for index, pair in [(i, p) for i in range(tokens // size) for p in range(pairs_here)]:
        rows = (pl.ds(index * size, size), pl.ds(pair * PAIR, PAIR))
        bias, bonus, gain = (ref[:, rows[1]] for ref in (bias_ref, bonus_ref, gain_ref))
        present = row_of + index * size < length
        rec = rec_ref[rows]
        key = jnp.where(present, key_ref[rows], 0.0)
        val = val_ref[rows].astype(BF16)
        total = jnp.where(present, -jnp.exp(bias + decay_ref[rows]), 0.0)
        scores = jnp.where(
            t_of == s_of,
            matmul_nt((rec * bonus).astype(BF16), by_head(key.astype(BF16), first_lanes)),
            0.0,
        )
        before = jnp.zeros_like(total)
        after = jnp.zeros_like(total)
        span = 1
        while span < size:
            later = (row_of & span) != 0
            scaled = (jnp.where(later, rec, key) * jnp.exp(jnp.where(later, before, after))).astype(
                BF16
            )
            pairs = matmul_nt(scaled, by_head(scaled, first_lanes))
            chosen = (
                ((t_of & span) != 0)
                & ((s_of & span) == 0)
                & ((t_of & (-2 * span)) == (s_of & (-2 * span)))
            )
            scores = jnp.where(chosen, pairs, scores)
            partner = jnp.where(
                later, pltpu.roll(total, span, 0), pltpu.roll(total, size - span, 0)
            )
            before = before + jnp.where(later, partner, 0.0)
            after = after + jnp.where(later, 0.0, partner)
            total = total + partner
            span *= 2
        state = held[pair]
        out = matmul(scores.astype(BF16), by_head(val, first_lanes))
        out = out + matmul_nt((rec * jnp.exp(before)).astype(BF16), state.astype(BF16))
        update = matmul_tn(val, (key * jnp.exp(after)).astype(BF16))
        held[pair] = state * jnp.exp(total[:1, :]) + jnp.where(own_head, update, 0.0)
        center = out - split_matmul(out, average)
        spread = split_matmul(center * center, average)
        grouped = center * lax.rsqrt(spread + 0.00064) * gain
        gate = gate_ref[rows]
        gated_ref[rows] = (grouped * (gate / (1.0 + jnp.exp(-gate)))).astype(BF16)
    for pair in range(pairs_here):
        final = held[pair].T
        final = final[:, :GROUP_DIMENSION] + final[:, GROUP_DIMENSION:]
        state_ref[2 * pair : 2 * pair + 2] = final.reshape(2, GROUP_DIMENSION, GROUP_DIMENSION)
    step = pl.program_id(0)
    width = exit_ref.shape[1]
    tile = min(1024, width)
    for first in range(0, width, tile):
        columns = slice(first, first + tile)
        part = matmul(gated_ref[...], exit_ref[:, columns])
        if steps == 1:
            terms_ref[:, columns] = part.astype(BF16)
            continue

        @pl.when(step == 0)
        def _():
            total_ref[:, columns] = part

        @pl.when((step > 0) & (step < steps - 1))
        def _():
            total_ref[:, columns] += part

        @pl.when(step == steps - 1)
        def _():
            terms_ref[:, columns] = (total_ref[:, columns] + part).astype(BF16)


def recurrence(length, base, values, far, decay, gate, bias, bonus, gain, start, exit_rows):
    tokens, width = decay.shape
    out_width = exit_rows.shape[1]
    together = min(2, width // PAIR)
    lanes = together * PAIR
    steps = width // lanes
    reach = sum(r.shape[0] * r.shape[2] for r in far) or 128
    place = values.shape[2] // reach - 1
    wide = pl.BlockSpec((tokens, lanes), lambda p: (0, p))
    row = pl.BlockSpec((1, lanes), lambda p: (0, p))
    states = pl.BlockSpec((2 * together, GROUP_DIMENSION, GROUP_DIMENSION), lambda p: (p, 0, 0))
    return pl.pallas_call(
        partial(recurrence_kernel, steps, len(far)),
        grid=(steps,),
        in_specs=[
            pl.BlockSpec(memory_space=pltpu.SMEM),
            pl.BlockSpec((3, tokens, lanes), lambda p: (0, 0, p)),
            pl.BlockSpec((3, tokens, reach), lambda p: (0, 0, place)),
        ]
        + [pl.BlockSpec((*r.shape[:3], lanes), lambda p: (0, 0, 0, p)) for r in far]
        + [wide] * 2
        + [row] * 3
        + [states, pl.BlockSpec((lanes, out_width), lambda p: (p, 0))],
        out_specs=[pl.BlockSpec((tokens, out_width), lambda p: (0, 0)), states],
        out_shape=[
            jax.ShapeDtypeStruct((tokens, out_width), BF16),
            jax.ShapeDtypeStruct(start.shape, F32),
        ],
        scratch_shapes=[
            pltpu.VMEM((together, PAIR, PAIR), F32),
            pltpu.VMEM((3, tokens, lanes), F32),
            pltpu.VMEM((tokens, lanes), BF16),
            pltpu.VMEM((tokens, out_width), F32),
        ],
        compiler_params=pltpu.CompilerParams(vmem_limit_bytes=44 << 20),
        cost_estimate=pl.CostEstimate(
            flops=1 << 20, bytes_accessed=24 * MICROSECOND, transcendentals=0
        ),
        name="recurrence",
    )(length, base, values, *far, decay, gate, bias, bonus, gain, start, exit_rows)


def prepare_kernel(
    order_ref,
    length_ref,
    tokens_ref,
    gain_ref,
    first_ref,
    mix_ref,
    stack_ref,
    out3_ref,
    out4_ref,
    last_ref,
    mean_ref,
    root_ref,
):
    step = pl.program_id(0)
    block = out3_ref.shape[1]
    seq_len, width = tokens_ref.shape

    @pl.when(step == 0)
    def _():
        count = min(64, seq_len)
        for index in range(seq_len // count):
            rows = pl.ds(index * count, count)
            values = tokens_ref[rows, :].astype(F32)
            mean = jnp.mean(values, axis=1, keepdims=True)
            center = values - mean
            spread = jnp.mean(center * center, axis=1, keepdims=True)
            mean_ref[rows, :] = jnp.broadcast_to(mean, (count, 128))
            root_ref[rows, :] = jnp.broadcast_to(lax.rsqrt(spread + 1e-05), (count, 128))

    columns = pl.ds(pl.multiple_of(order_ref[step] * block, block), block)
    values = tokens_ref[:, columns].astype(F32)
    normed = (values - mean_ref[:, :1]) * root_ref[:, :1] * gain_ref[:1, columns]
    places = lax.broadcasted_iota(jnp.int32, normed.shape, 0)
    before = jnp.where(places == 0, first_ref[:1, columns], pltpu.roll(normed, 1, 0))
    change = before - normed
    outs = [stack_ref.at[0], stack_ref.at[1], stack_ref.at[2], out3_ref, out4_ref]
    for m, out_ref in enumerate(outs):
        out_ref[...] = (normed + change * mix_ref[m : m + 1, columns]).astype(BF16)
    last = places == length_ref[0] - 1
    last_ref[...] = jnp.sum(jnp.where(last, normed, 0.0), axis=0, keepdims=True)


def prepare(order, length, tokens, gain, first, mixes):
    seq_len, width = tokens.shape
    blocks = order.shape[0]
    block = width // blocks

    def rows(count):
        return pl.BlockSpec((count, width), lambda j, *_: (0, 0))

    moved = pl.BlockSpec((3, seq_len, block), lambda j, *_: (0, 0, j))
    natural = pl.BlockSpec((seq_len, block), lambda j, order, *_: (0, order[j]))
    return pl.pallas_call(
        prepare_kernel,
        grid_spec=pltpu.PrefetchScalarGridSpec(
            num_scalar_prefetch=2,
            grid=(blocks,),
            in_specs=[rows(seq_len), rows(1), rows(1), rows(mixes.shape[0])],
            out_specs=[moved]
            + [natural] * 2
            + [pl.BlockSpec((1, block), lambda j, order, *_: (0, order[j]))],
            scratch_shapes=[pltpu.VMEM((seq_len, 128), F32)] * 2,
        ),
        out_shape=[jax.ShapeDtypeStruct((3, seq_len, width), BF16)]
        + [jax.ShapeDtypeStruct((seq_len, width), BF16)] * 2
        + [jax.ShapeDtypeStruct((1, width), F32)],
        compiler_params=pltpu.CompilerParams(vmem_limit_bytes=VMEM_BYTES),
        cost_estimate=pl.CostEstimate(
            flops=1 << 20, bytes_accessed=22 * MICROSECOND, transcendentals=0
        ),
        name="prepare",
    )(order, length, tokens, gain, first, mixes)


def regroup_kernel(*refs):
    out_ref = refs[-1]
    rows = refs[0].shape[0]
    count, _, wide = out_ref.shape
    for at, piece_ref in enumerate(refs[:-1]):
        for h in range(count):
            block = piece_ref[:, h * wide : (h + 1) * wide]
            out_ref[h, at * rows : (at + 1) * rows, :] = block.astype(BF16)


def regroup(pieces, hid):
    rows, width = pieces[0].shape
    wide = width // hid
    tall = rows * len(pieces)
    steps = 4
    return pl.pallas_call(
        regroup_kernel,
        grid=(steps,),
        in_specs=[pl.BlockSpec((rows, width // steps), lambda h: (0, h))] * len(pieces),
        out_specs=pl.BlockSpec((hid // steps, tall, wide), lambda h: (h, 0, 0)),
        out_shape=jax.ShapeDtypeStruct((hid, tall, wide), BF16),
        compiler_params=pltpu.CompilerParams(vmem_limit_bytes=VMEM_BYTES),
        cost_estimate=pl.CostEstimate(flops=0, bytes_accessed=20 << 20, transcendentals=0),
        name="regroup",
    )(*pieces)


def rows_product(total, values_ref, m, rows):
    first = 0
    for rows_ref in rows:
        block = rows_ref[:, m]
        span = block.shape[0] * block.shape[1]
        values = values_ref[m, :, first : first + span]
        total = total + matmul(values, block.reshape(span, block.shape[2]))
        first += span
    return total


def project_kernel(values_ref, *refs):
    refs[-1][0] = rows_product(0.0, values_ref, 0, refs[:-1])


def project(values, rows):
    count, tokens, width = values.shape
    wide = rows[0].shape[-1]
    tile = min(256, wide)
    out = pl.BlockSpec((1, tokens, tile), lambda m, n: (m, 0, n))
    return pl.pallas_call(
        project_kernel,
        grid=(count, wide // tile),
        in_specs=[pl.BlockSpec((1, tokens, width), lambda m, n: (m, 0, 0))]
        + [
            pl.BlockSpec((r.shape[0], 1, r.shape[2], tile), lambda m, n: (0, m, 0, n))
            for r in rows
        ],
        out_specs=out,
        out_shape=jax.ShapeDtypeStruct((count, tokens, wide), F32),
        compiler_params=pltpu.CompilerParams(vmem_limit_bytes=VMEM_BYTES),
        cost_estimate=pl.CostEstimate(
            flops=1 << 20, bytes_accessed=13 * MICROSECOND, transcendentals=0
        ),
        name="project",
    )(values, *rows)


def channel_kernel(places, steps, length_ref, tokens_ref, attended_ref, gain_ref, first_ref, mix_ref, *refs):
    count = len(places)
    rows, refs = refs[:count], refs[count:]
    hidden_ref, accept_ref, last_ref, held, mixed, taken, arrived = refs
    step = pl.program_id(0)
    copies = [
        pltpu.make_async_copy(ref, taken.at[pl.ds(first, ref.shape[0]), :], arrived.at[at])
        for at, (ref, first) in enumerate(zip(rows, places))
    ]

    @pl.when(step == 0)
    def _():
        for copy in copies:
            copy.start()
        held[...] = first_ref[...]
        last_ref[...] = jnp.zeros_like(last_ref)

    middle = (tokens_ref[...].astype(F32) + attended_ref[...].astype(F32)).astype(BF16)
    values = middle.astype(F32)
    center = values - jnp.mean(values, axis=1, keepdims=True)
    spread = jnp.mean(center * center, axis=1, keepdims=True)
    normed = center * lax.rsqrt(spread + 1e-05) * gain_ref[...]
    tall = normed.shape[0]
    row_of = lax.broadcasted_iota(jnp.int32, normed.shape, 0)
    before = jnp.where(row_of == 0, held[...], pltpu.roll(normed, 1, 0))
    held[...] = normed[tall - 1 :, :]
    change = before - normed
    mixed[pl.ds(pl.multiple_of(step * tall, tall), tall), :] = (
        normed + change * mix_ref[:1, :]
    ).astype(BF16)
    accept_ref[...] = (normed + change * mix_ref[1:2, :]).astype(BF16)
    place = length_ref[0] - 1 - step * tall

    @pl.when((place >= 0) & (place < tall))
    def _():
        last_ref[...] = jnp.sum(jnp.where(row_of == place, normed, 0.0), axis=0, keepdims=True)

    @pl.when(step == steps - 1)
    def _():
        units = hidden_ref.shape[1]
        ready = 0
        for first in range(0, units, 256):
            end = min(first + 256, units)
            while ready < count and places[ready] < end:
                copies[ready].wait()
                ready += 1
            inner = jnp.maximum(matmul_nt(mixed[...], taken[first:end, :]), 0.0)
            hidden_ref[:, first:end] = (inner * inner).astype(BF16)


def channel_inputs(length, tokens, attended, gain, first, mixes, rows):
    seq_len, width = tokens.shape
    tall = min(128, seq_len)
    steps = seq_len // tall
    by_rows = pl.BlockSpec((tall, width), lambda i: (i, 0))
    places = [0]
    for block in rows:
        places.append(places[-1] + block.shape[0])

    def wide(number):
        return pl.BlockSpec((number, width), lambda i: (0, 0))

    return pl.pallas_call(
        partial(channel_kernel, places[:-1], steps),
        grid=(steps,),
        in_specs=[
            pl.BlockSpec(memory_space=pltpu.SMEM),
            by_rows,
            by_rows,
            wide(1),
            wide(1),
            wide(2),
        ]
        + [pl.BlockSpec(memory_space=pl.ANY)] * len(rows),
        out_specs=[
            pl.BlockSpec((seq_len, places[-1]), lambda i: (0, 0)),
            by_rows,
            wide(1),
        ],
        out_shape=[
            jax.ShapeDtypeStruct((seq_len, places[-1]), BF16),
            jax.ShapeDtypeStruct((seq_len, width), BF16),
            jax.ShapeDtypeStruct((1, width), F32),
        ],
        scratch_shapes=[
            pltpu.VMEM((1, width), F32),
            pltpu.VMEM((seq_len, width), BF16),
            pltpu.VMEM((places[-1], width), BF16),
            pltpu.SemaphoreType.DMA((len(rows),)),
        ],
        compiler_params=pltpu.CompilerParams(vmem_limit_bytes=VMEM_BYTES),
        cost_estimate=pl.CostEstimate(
            flops=1 << 20, bytes_accessed=22 * MICROSECOND, transcendentals=0
        ),
        name="channel_inputs",
    )(length, tokens, attended, gain, first, mixes, *rows)


def exit_kernel(hidden_ref, *refs):
    values = jnp.concatenate([ref[...] for ref in refs[:-1]], axis=0)
    refs[-1][...] = matmul(hidden_ref[...], values).astype(BF16)


def exit_product(hidden, values):
    tokens = hidden.shape[0]
    width = values[0].shape[1]
    tile = min(1024, width)
    return pl.pallas_call(
        exit_kernel,
        grid=(width // tile,),
        in_specs=[pl.BlockSpec(hidden.shape, lambda n: (0, 0))]
        + [pl.BlockSpec((v.shape[0], tile), lambda n: (0, n)) for v in values],
        out_specs=pl.BlockSpec((tokens, tile), lambda n: (0, n)),
        out_shape=jax.ShapeDtypeStruct((tokens, width), BF16),
        compiler_params=pltpu.CompilerParams(vmem_limit_bytes=VMEM_BYTES),
        cost_estimate=pl.CostEstimate(
            flops=1 << 20, bytes_accessed=7 * MICROSECOND, transcendentals=0
        ),
        name="exit_product",
    )(hidden, *values)


def combine_kernel(slot_ref, length_ref, tokens_ref, attended_ref, gate_ref, *refs):
    out_ref = refs[-1]
    present = lax.broadcasted_iota(jnp.int32, gate_ref.shape, 0) < length_ref[0]
    summed = jnp.concatenate([ref[...] for ref in refs[:-1]], axis=1).astype(F32)
    accept = 1.0 / (1.0 + jnp.exp(-gate_ref[...]))
    middle = (tokens_ref[...].astype(F32) + attended_ref[...].astype(F32)).astype(BF16)
    combined = middle.astype(F32) + accept * summed
    out_ref[...] = jnp.where(present, combined, 0.0).astype(BF16)


def combine(slot, length, tokens, attended, gate, summed):
    seq_len, wide = gate.shape
    whole = pl.BlockSpec((seq_len, wide), lambda i, *_: (0, 0))
    parts = [pl.BlockSpec(part.shape, lambda i, *_: (0, 0)) for part in summed]
    return pl.pallas_call(
        combine_kernel,
        grid_spec=pltpu.PrefetchScalarGridSpec(
            num_scalar_prefetch=2,
            grid=(1,),
            in_specs=[pl.BlockSpec((seq_len, wide), lambda i, slot, *_: (0, slot[0]))] * 2
            + [whole]
            + parts,
            out_specs=whole,
        ),
        out_shape=jax.ShapeDtypeStruct((seq_len, wide), BF16),
        compiler_params=pltpu.CompilerParams(vmem_limit_bytes=VMEM_BYTES),
        cost_estimate=pl.CostEstimate(
            flops=1 << 20, bytes_accessed=3 * MICROSECOND, transcendentals=0
        ),
        name="combine",
    )(slot, length, tokens, attended, gate, *summed)


def local(
    input_activations,
    prompt_extents,
    continuing_flags,
    owning_index,
    partition_arrangement,
    training_accept_pieces,
    training_lookup_pieces,
    training_content_pieces,
    normalizer_scales,
    prior_step_blends,
    forgetting_bias_vector,
    forgetting_left_lowrank,
    forgetting_right_lowrank,
    instant_emphasis,
    group_normalizer_scale,
    gating_projection,
    mixing_exit_projection,
    kept_summary_places,
    previous_normed_entries,
    feedforward_entry_proj,
    feedforward_exit_proj,
    feedforward_accept_proj,
):
    hid = lax.axis_size("hid")
    req = lax.axis_size("req")
    here = lax.axis_index("req")
    slot = lax.axis_index("hid")
    token_rows = input_activations[0]
    seq_len, width = token_rows.shape
    local_width = mixing_exit_projection.shape[0]
    heads = local_width // GROUP_DIMENSION
    shards = partition_arrangement.shape[0]
    shard_rows = width // shards
    length = prompt_extents[0]
    resuming = continuing_flags[0]

    owned = (resuming == 1) & (owning_index[0] == slot)
    saved = jnp.where(owned, kept_summary_places[0, 0].astype(BF16), 0)
    start = lax.psum_scatter(
        saved.reshape(saved.shape[0], -1), "hid", scatter_dimension=0, tiled=True
    )
    start = start.astype(F32).reshape(heads, GROUP_DIMENSION, GROUP_DIMENSION)

    order = jnp.concatenate(
        [
            lax.dynamic_slice_in_dim(partition_arrangement, (here ^ d) * hid, hid, 0)
            for d in range(req)
        ]
    )
    gain_rows = normalizer_scales.astype(F32)
    mix_rows = prior_step_blends.astype(F32)
    carried = jnp.where(resuming == 1, previous_normed_entries[0].astype(F32), 0.0)
    if shard_rows % 128 == 0:
        blended, decay_in, gate_in, last_in = prepare(
            order, prompt_extents, token_rows, gain_rows[:1], carried[:1], mix_rows[:5]
        )
    else:
        normed_in = layer_norm(token_rows.astype(F32), gain_rows[0])
        before = shifted(normed_in, carried[0])
        rec_in, key_in, val_in, decay_in, gate_in = [
            (normed_in + (before - normed_in) * mix_rows[m][None, :]).astype(BF16)
            for m in range(5)
        ]
        blended = jnp.stack([rec_in, key_in, val_in]).reshape(3, seq_len, shards, shard_rows)
        blended = jnp.take(blended, order, axis=2).reshape(3, seq_len, width)
        last_in = lax.dynamic_slice_in_dim(normed_in, length - 1, 1, 0)

    def side_products(decay_in, gate_in):
        low_rank = jnp.tanh(matmul(decay_in, forgetting_left_lowrank)).astype(BF16)
        return matmul(low_rank, forgetting_right_lowrank), matmul(gate_in, gating_projection)

    def to_heads(columns):
        mine = lax.all_to_all(columns, "hid", split_axis=0, concat_axis=0, tiled=True)
        mine = mine.reshape(hid, -1, shard_rows, local_width)
        return [mine[: hid // 2], mine[hid // 2 :]]

    columns = regroup(
        [training_accept_pieces, training_lookup_pieces, training_content_pieces], hid
    )
    units = feedforward_entry_proj.shape[0]
    hold = lax.optimization_barrier
    if req == 4:
        half = units // 2
        cut = half * 5 // 7 // 16 * 16
        key_mine, value_mine = feedforward_entry_proj, feedforward_exit_proj
        key_x, key_y = across(key_mine, 1), across(key_mine, 2)
        mine = to_heads(columns)
        decay, gate = side_products(decay_in, gate_in)
        mine, key_x, key_y, blended, decay, gate, start = hold(
            (mine, key_x, key_y, blended, decay, gate, start)
        )
        trained = [mine, [across(rows, 1) for rows in mine], [across(rows, 2) for rows in mine]]
        first = [key_x[:cut], key_y[half : half + cut]]
        second = [key_x[cut:half], key_y[half + cut :]]
        trained, first, second = hold((trained, first, second))
        opposite = [across(trained[1][0], 2), across(trained[2][1], 1)]
        projected = project(blended, sum(trained, []))
        projected, opposite, first = hold((projected, opposite, first))
        key_far = [across(first[0], 2), across(first[1], 1)]
    else:
        decay, gate = side_products(decay_in, gate_in)
        low, high = [whole(side, req) for side in to_heads(columns)]
        opposite = []
        projected = project(blended, [side[d] for d in range(req) for side in (low, high)])
    head_terms, new_state = recurrence(
        prompt_extents,
        projected,
        blended,
        opposite,
        decay,
        gate,
        forgetting_bias_vector[None],
        instant_emphasis[None],
        group_normalizer_scale[None],
        start,
        mixing_exit_projection,
    )
    if req == 4:
        head_terms, value_mine, second, key_far = hold(
            (head_terms, value_mine, second, key_far)
        )
    attended = lax.psum(head_terms, "hid")
    if req == 4:
        value_x, value_y = across(value_mine, 1), across(value_mine, 2)
        key_far.insert(1, across(second[0], 2))
        key_far.append(across(second[1], 1))
        value_far = [value_x[:half], value_y[half:]]
        value_far, key_far = hold((value_far, key_far))
        value_far = [across(value_far[0], 2), across(value_far[1], 1)]
        key_rows = [key_mine, key_x, key_y, *key_far]
        value_rows = [value_mine, value_x, value_y, *value_far]
    else:
        key_rows = whole(feedforward_entry_proj, req)
        value_rows = whole(feedforward_exit_proj, req)
    hidden, accept_in, last_chan = channel_inputs(
        prompt_extents,
        token_rows,
        attended,
        gain_rows[1:],
        carried[1:],
        mix_rows[5:],
        key_rows,
    )
    accept = matmul(accept_in, feedforward_accept_proj)
    terms = exit_product(hidden, value_rows)
    summed = lax.psum_scatter(terms, "hid", scatter_dimension=1, tiled=True)
    layer_out = combine(
        slot[None], prompt_extents, token_rows, attended, accept, [summed]
    )[None]
    shift_out = jnp.concatenate([last_in, last_chan]).astype(BF16)[None]
    return (layer_out, new_state[None], shift_out)


def solution(mesh):
    placed = (
        P("req", None, None),
        P("req"),
        P("req"),
        P("req"),
        P(),
        P(("req", "hid"), None),
        P(("req", "hid"), None),
        P(("req", "hid"), None),
        P(),
        P(),
        P("hid"),
        P(),
        P(None, "hid"),
        P("hid"),
        P("hid"),
        P(None, "hid"),
        P("hid", None),
        P("req", "hid", None, None, None),
        P("req", None, None),
        P(("req", "hid"), None),
        P(("req", "hid"), None),
        P(None, "hid"),
    )
    return jax.shard_map(
        local,
        mesh=mesh,
        in_specs=placed,
        out_specs=(P("req", None, "hid"), P("req", "hid", None, None), P("req", None, None)),
        check_vma=False,
    )
```

```python
from functools import partial

import jax
import jax.numpy as jnp
from jax import lax
from jax.experimental import pallas as pl
from jax.experimental.pallas import tpu as pltpu
from jax.sharding import PartitionSpec as P

GROUP_DIMENSION = 64
PAIR = 2 * GROUP_DIMENSION
CHUNK = 64
BF16 = jnp.bfloat16
F32 = jnp.float32
MICROSECOND = 3690000
VMEM_BYTES = 60 << 20


def layer_norm(values, gain):
    center = values - jnp.mean(values, axis=-1, keepdims=True)
    spread = jnp.mean(center * center, axis=-1, keepdims=True)
    return center / jnp.sqrt(spread + 1e-05) * gain


def shifted(values, first_row):
    return jnp.concatenate([first_row[None, :], values[:-1]], axis=0)


def matmul(a, b):
    return jnp.dot(a, b, preferred_element_type=F32)


def matmul_nt(a, b):
    return lax.dot_general(a, b, (((1,), (1,)), ((), ())), preferred_element_type=F32)


def matmul_tn(a, b):
    return lax.dot_general(a, b, (((0,), (0,)), ((), ())), preferred_element_type=F32)


def across(value, axis):
    return lax.ppermute(value, "req", [(i, i ^ axis) for i in range(4)])


def whole(value, req):
    blocks = lax.all_gather(value, "req", axis=0, tiled=False)
    me = lax.axis_index("req")
    return [lax.dynamic_index_in_dim(blocks, me ^ d, 0, keepdims=False) for d in range(req)]


def by_head(values, first_lanes):
    zeros = jnp.zeros_like(values)
    return jnp.concatenate(
        [jnp.where(first_lanes, values, zeros), jnp.where(first_lanes, zeros, values)], axis=0
    )


def split_matmul(values, weights):
    high = values.astype(BF16)
    low = (values - high.astype(F32)).astype(BF16)
    return matmul(high, weights) + matmul(low, weights)


def recurrence_kernel(
    steps,
    count,
    length_ref,
    base_ref,
    values_ref,
    *refs,
):
    rows_far, refs = refs[:count], refs[count:]
    decay_ref, gate_ref, bias_ref, bonus_ref, gain_ref, start_ref, exit_ref = refs[:7]
    terms_ref, state_ref, held, projected, gated_ref, total_ref = refs[7:]
    rec_ref, key_ref, val_ref = (projected.at[m] for m in range(3))
    for m in range(3):
        projected[m] = rows_product(base_ref[m], values_ref, m, rows_far)
    length = length_ref[0]
    tokens = base_ref.shape[1]
    size = min(CHUNK, tokens)
    lanes = lax.broadcasted_iota(jnp.int32, (size, PAIR), 1)
    first_lanes = lanes < GROUP_DIMENSION
    row_of = lax.broadcasted_iota(jnp.int32, (size, PAIR), 0)
    t_of = lax.broadcasted_iota(jnp.int32, (size, 2 * size), 0)
    s_of = lax.broadcasted_iota(jnp.int32, (size, 2 * size), 1) & (size - 1)
    side_a = lax.broadcasted_iota(jnp.int32, (PAIR, PAIR), 0) < GROUP_DIMENSION
    side_b = lax.broadcasted_iota(jnp.int32, (PAIR, PAIR), 1) < GROUP_DIMENSION
    own_head = side_a == side_b
    average = jnp.where(own_head, 1.0 / GROUP_DIMENSION, 0.0).astype(BF16)
    pairs_here = base_ref.shape[2] // PAIR
    for pair in range(pairs_here):
        start = start_ref[2 * pair : 2 * pair + 2].reshape(PAIR, GROUP_DIMENSION)
        start = jnp.where(own_head, jnp.concatenate([start, start], axis=1), 0.0)
        held[pair] = start.T
    for index, pair in [(i, p) for i in range(tokens // size) for p in range(pairs_here)]:
        rows = (pl.ds(index * size, size), pl.ds(pair * PAIR, PAIR))
        bias, bonus, gain = (ref[:, rows[1]] for ref in (bias_ref, bonus_ref, gain_ref))
        present = row_of + index * size < length
        rec = rec_ref[rows]
        key = jnp.where(present, key_ref[rows], 0.0)
        val = val_ref[rows].astype(BF16)
        total = jnp.where(present, -jnp.exp(bias + decay_ref[rows]), 0.0)
        scores = jnp.where(
            t_of == s_of,
            matmul_nt((rec * bonus).astype(BF16), by_head(key.astype(BF16), first_lanes)),
            0.0,
        )
        before = jnp.zeros_like(total)
        after = jnp.zeros_like(total)
        span = 1
        while span < size:
            later = (row_of & span) != 0
            scaled = (jnp.where(later, rec, key) * jnp.exp(jnp.where(later, before, after))).astype(
                BF16
            )
            pairs = matmul_nt(scaled, by_head(scaled, first_lanes))
            chosen = (
                ((t_of & span) != 0)
                & ((s_of & span) == 0)
                & ((t_of & (-2 * span)) == (s_of & (-2 * span)))
            )
            scores = jnp.where(chosen, pairs, scores)
            partner = jnp.where(
                later, pltpu.roll(total, span, 0), pltpu.roll(total, size - span, 0)
            )
            before = before + jnp.where(later, partner, 0.0)
            after = after + jnp.where(later, 0.0, partner)
            total = total + partner
            span *= 2
        state = held[pair]
        out = matmul(scores.astype(BF16), by_head(val, first_lanes))
        out = out + matmul_nt((rec * jnp.exp(before)).astype(BF16), state.astype(BF16))
        update = matmul_tn(val, (key * jnp.exp(after)).astype(BF16))
        held[pair] = state * jnp.exp(total[:1, :]) + jnp.where(own_head, update, 0.0)
        center = out - split_matmul(out, average)
        spread = split_matmul(center * center, average)
        grouped = center * lax.rsqrt(spread + 0.00064) * gain
        gate = gate_ref[rows]
        gated_ref[rows] = (grouped * (gate / (1.0 + jnp.exp(-gate)))).astype(BF16)
    for pair in range(pairs_here):
        final = held[pair].T
        final = final[:, :GROUP_DIMENSION] + final[:, GROUP_DIMENSION:]
        state_ref[2 * pair : 2 * pair + 2] = final.reshape(2, GROUP_DIMENSION, GROUP_DIMENSION)
    step = pl.program_id(0)
    width = exit_ref.shape[1]
    tile = min(1024, width)
    for first in range(0, width, tile):
        columns = slice(first, first + tile)
        part = matmul(gated_ref[...], exit_ref[:, columns])
        if steps == 1:
            terms_ref[:, columns] = part.astype(BF16)
            continue

        @pl.when(step == 0)
        def _():
            total_ref[:, columns] = part

        @pl.when((step > 0) & (step < steps - 1))
        def _():
            total_ref[:, columns] += part

        @pl.when(step == steps - 1)
        def _():
            terms_ref[:, columns] = (total_ref[:, columns] + part).astype(BF16)


def recurrence(length, base, values, far, decay, gate, bias, bonus, gain, start, exit_rows):
    tokens, width = decay.shape
    out_width = exit_rows.shape[1]
    together = min(2, width // PAIR)
    lanes = together * PAIR
    steps = width // lanes
    reach = sum(r.shape[0] * r.shape[2] for r in far) or 128
    place = values.shape[2] // reach - 1
    wide = pl.BlockSpec((tokens, lanes), lambda p: (0, p))
    row = pl.BlockSpec((1, lanes), lambda p: (0, p))
    states = pl.BlockSpec((2 * together, GROUP_DIMENSION, GROUP_DIMENSION), lambda p: (p, 0, 0))
    return pl.pallas_call(
        partial(recurrence_kernel, steps, len(far)),
        grid=(steps,),
        in_specs=[
            pl.BlockSpec(memory_space=pltpu.SMEM),
            pl.BlockSpec((3, tokens, lanes), lambda p: (0, 0, p)),
            pl.BlockSpec((3, tokens, reach), lambda p: (0, 0, place)),
        ]
        + [pl.BlockSpec((*r.shape[:3], lanes), lambda p: (0, 0, 0, p)) for r in far]
        + [wide] * 2
        + [row] * 3
        + [states, pl.BlockSpec((lanes, out_width), lambda p: (p, 0))],
        out_specs=[pl.BlockSpec((tokens, out_width), lambda p: (0, 0)), states],
        out_shape=[
            jax.ShapeDtypeStruct((tokens, out_width), BF16),
            jax.ShapeDtypeStruct(start.shape, F32),
        ],
        scratch_shapes=[
            pltpu.VMEM((together, PAIR, PAIR), F32),
            pltpu.VMEM((3, tokens, lanes), F32),
            pltpu.VMEM((tokens, lanes), BF16),
            pltpu.VMEM((tokens, out_width), F32),
        ],
        compiler_params=pltpu.CompilerParams(vmem_limit_bytes=44 << 20),
        cost_estimate=pl.CostEstimate(
            flops=1 << 20, bytes_accessed=24 * MICROSECOND, transcendentals=0
        ),
        name="recurrence",
    )(length, base, values, *far, decay, gate, bias, bonus, gain, start, exit_rows)


def prepare_kernel(
    order_ref,
    length_ref,
    tokens_ref,
    gain_ref,
    first_ref,
    mix_ref,
    stack_ref,
    out3_ref,
    out4_ref,
    last_ref,
    mean_ref,
    root_ref,
):
    step = pl.program_id(0)
    block = out3_ref.shape[1]
    seq_len, width = tokens_ref.shape

    @pl.when(step == 0)
    def _():
        count = min(64, seq_len)
        for index in range(seq_len // count):
            rows = pl.ds(index * count, count)
            values = tokens_ref[rows, :].astype(F32)
            mean = jnp.mean(values, axis=1, keepdims=True)
            center = values - mean
            spread = jnp.mean(center * center, axis=1, keepdims=True)
            mean_ref[rows, :] = jnp.broadcast_to(mean, (count, 128))
            root_ref[rows, :] = jnp.broadcast_to(lax.rsqrt(spread + 1e-05), (count, 128))

    columns = pl.ds(pl.multiple_of(order_ref[step] * block, block), block)
    values = tokens_ref[:, columns].astype(F32)
    normed = (values - mean_ref[:, :1]) * root_ref[:, :1] * gain_ref[:1, columns]
    places = lax.broadcasted_iota(jnp.int32, normed.shape, 0)
    before = jnp.where(places == 0, first_ref[:1, columns], pltpu.roll(normed, 1, 0))
    change = before - normed
    outs = [stack_ref.at[0], stack_ref.at[1], stack_ref.at[2], out3_ref, out4_ref]
    for m, out_ref in enumerate(outs):
        out_ref[...] = (normed + change * mix_ref[m : m + 1, columns]).astype(BF16)
    last = places == length_ref[0] - 1
    last_ref[...] = jnp.sum(jnp.where(last, normed, 0.0), axis=0, keepdims=True)


def prepare(order, length, tokens, gain, first, mixes):
    seq_len, width = tokens.shape
    blocks = order.shape[0]
    block = width // blocks

    def rows(count):
        return pl.BlockSpec((count, width), lambda j, *_: (0, 0))

    moved = pl.BlockSpec((3, seq_len, block), lambda j, *_: (0, 0, j))
    natural = pl.BlockSpec((seq_len, block), lambda j, order, *_: (0, order[j]))
    return pl.pallas_call(
        prepare_kernel,
        grid_spec=pltpu.PrefetchScalarGridSpec(
            num_scalar_prefetch=2,
            grid=(blocks,),
            in_specs=[rows(seq_len), rows(1), rows(1), rows(mixes.shape[0])],
            out_specs=[moved]
            + [natural] * 2
            + [pl.BlockSpec((1, block), lambda j, order, *_: (0, order[j]))],
            scratch_shapes=[pltpu.VMEM((seq_len, 128), F32)] * 2,
        ),
        out_shape=[jax.ShapeDtypeStruct((3, seq_len, width), BF16)]
        + [jax.ShapeDtypeStruct((seq_len, width), BF16)] * 2
        + [jax.ShapeDtypeStruct((1, width), F32)],
        compiler_params=pltpu.CompilerParams(vmem_limit_bytes=VMEM_BYTES),
        cost_estimate=pl.CostEstimate(
            flops=1 << 20, bytes_accessed=22 * MICROSECOND, transcendentals=0
        ),
        name="prepare",
    )(order, length, tokens, gain, first, mixes)


def regroup_kernel(*refs):
    out_ref = refs[-1]
    rows = refs[0].shape[0]
    count, _, wide = out_ref.shape
    for at, piece_ref in enumerate(refs[:-1]):
        for h in range(count):
            block = piece_ref[:, h * wide : (h + 1) * wide]
            out_ref[h, at * rows : (at + 1) * rows, :] = block.astype(BF16)


def regroup(pieces, hid):
    rows, width = pieces[0].shape
    wide = width // hid
    tall = rows * len(pieces)
    steps = 4
    return pl.pallas_call(
        regroup_kernel,
        grid=(steps,),
        in_specs=[pl.BlockSpec((rows, width // steps), lambda h: (0, h))] * len(pieces),
        out_specs=pl.BlockSpec((hid // steps, tall, wide), lambda h: (h, 0, 0)),
        out_shape=jax.ShapeDtypeStruct((hid, tall, wide), BF16),
        compiler_params=pltpu.CompilerParams(vmem_limit_bytes=VMEM_BYTES),
        cost_estimate=pl.CostEstimate(flops=0, bytes_accessed=20 << 20, transcendentals=0),
        name="regroup",
    )(*pieces)


def rows_product(total, values_ref, m, rows):
    first = 0
    for rows_ref in rows:
        block = rows_ref[:, m]
        span = block.shape[0] * block.shape[1]
        values = values_ref[m, :, first : first + span]
        total = total + matmul(values, block.reshape(span, block.shape[2]))
        first += span
    return total


def project_kernel(values_ref, *refs):
    refs[-1][0] = rows_product(0.0, values_ref, 0, refs[:-1])


def project(values, rows):
    count, tokens, width = values.shape
    wide = rows[0].shape[-1]
    tile = min(256, wide)
    out = pl.BlockSpec((1, tokens, tile), lambda m, n: (m, 0, n))
    return pl.pallas_call(
        project_kernel,
        grid=(count, wide // tile),
        in_specs=[pl.BlockSpec((1, tokens, width), lambda m, n: (m, 0, 0))]
        + [
            pl.BlockSpec((r.shape[0], 1, r.shape[2], tile), lambda m, n: (0, m, 0, n))
            for r in rows
        ],
        out_specs=out,
        out_shape=jax.ShapeDtypeStruct((count, tokens, wide), F32),
        compiler_params=pltpu.CompilerParams(vmem_limit_bytes=VMEM_BYTES),
        cost_estimate=pl.CostEstimate(
            flops=1 << 20, bytes_accessed=13 * MICROSECOND, transcendentals=0
        ),
        name="project",
    )(values, *rows)


def channel_kernel(places, steps, length_ref, tokens_ref, attended_ref, gain_ref, first_ref, mix_ref, *refs):
    count = len(places)
    rows, refs = refs[:count], refs[count:]
    hidden_ref, accept_ref, last_ref, held, mixed, taken, arrived = refs
    step = pl.program_id(0)
    copies = [
        pltpu.make_async_copy(ref, taken.at[pl.ds(first, ref.shape[0]), :], arrived.at[at])
        for at, (ref, first) in enumerate(zip(rows, places))
    ]

    @pl.when(step == 0)
    def _():
        for copy in copies:
            copy.start()
        held[...] = first_ref[...]
        last_ref[...] = jnp.zeros_like(last_ref)

    middle = (tokens_ref[...].astype(F32) + attended_ref[...].astype(F32)).astype(BF16)
    values = middle.astype(F32)
    center = values - jnp.mean(values, axis=1, keepdims=True)
    spread = jnp.mean(center * center, axis=1, keepdims=True)
    normed = center * lax.rsqrt(spread + 1e-05) * gain_ref[...]
    tall = normed.shape[0]
    row_of = lax.broadcasted_iota(jnp.int32, normed.shape, 0)
    before = jnp.where(row_of == 0, held[...], pltpu.roll(normed, 1, 0))
    held[...] = normed[tall - 1 :, :]
    change = before - normed
    mixed[pl.ds(pl.multiple_of(step * tall, tall), tall), :] = (
        normed + change * mix_ref[:1, :]
    ).astype(BF16)
    accept_ref[...] = (normed + change * mix_ref[1:2, :]).astype(BF16)
    place = length_ref[0] - 1 - step * tall

    @pl.when((place >= 0) & (place < tall))
    def _():
        last_ref[...] = jnp.sum(jnp.where(row_of == place, normed, 0.0), axis=0, keepdims=True)

    @pl.when(step == steps - 1)
    def _():
        units = hidden_ref.shape[1]
        ready = 0
        for first in range(0, units, 256):
            end = min(first + 256, units)
            while ready < count and places[ready] < end:
                copies[ready].wait()
                ready += 1
            inner = jnp.maximum(matmul_nt(mixed[...], taken[first:end, :]), 0.0)
            hidden_ref[:, first:end] = (inner * inner).astype(BF16)


def channel_inputs(length, tokens, attended, gain, first, mixes, rows):
    seq_len, width = tokens.shape
    tall = min(128, seq_len)
    steps = seq_len // tall
    by_rows = pl.BlockSpec((tall, width), lambda i: (i, 0))
    places = [0]
    for block in rows:
        places.append(places[-1] + block.shape[0])

    def wide(number):
        return pl.BlockSpec((number, width), lambda i: (0, 0))

    return pl.pallas_call(
        partial(channel_kernel, places[:-1], steps),
        grid=(steps,),
        in_specs=[
            pl.BlockSpec(memory_space=pltpu.SMEM),
            by_rows,
            by_rows,
            wide(1),
            wide(1),
            wide(2),
        ]
        + [pl.BlockSpec(memory_space=pl.ANY)] * len(rows),
        out_specs=[
            pl.BlockSpec((seq_len, places[-1]), lambda i: (0, 0)),
            by_rows,
            wide(1),
        ],
        out_shape=[
            jax.ShapeDtypeStruct((seq_len, places[-1]), BF16),
            jax.ShapeDtypeStruct((seq_len, width), BF16),
            jax.ShapeDtypeStruct((1, width), F32),
        ],
        scratch_shapes=[
            pltpu.VMEM((1, width), F32),
            pltpu.VMEM((seq_len, width), BF16),
            pltpu.VMEM((places[-1], width), BF16),
            pltpu.SemaphoreType.DMA((len(rows),)),
        ],
        compiler_params=pltpu.CompilerParams(vmem_limit_bytes=VMEM_BYTES),
        cost_estimate=pl.CostEstimate(
            flops=1 << 20, bytes_accessed=22 * MICROSECOND, transcendentals=0
        ),
        name="channel_inputs",
    )(length, tokens, attended, gain, first, mixes, *rows)


def exit_kernel(hidden_ref, *refs):
    values = jnp.concatenate([ref[...] for ref in refs[:-1]], axis=0)
    refs[-1][...] = matmul(hidden_ref[...], values).astype(BF16)


def exit_product(hidden, values):
    tokens = hidden.shape[0]
    width = values[0].shape[1]
    tile = min(1024, width)
    return pl.pallas_call(
        exit_kernel,
        grid=(width // tile,),
        in_specs=[pl.BlockSpec(hidden.shape, lambda n: (0, 0))]
        + [pl.BlockSpec((v.shape[0], tile), lambda n: (0, n)) for v in values],
        out_specs=pl.BlockSpec((tokens, tile), lambda n: (0, n)),
        out_shape=jax.ShapeDtypeStruct((tokens, width), BF16),
        compiler_params=pltpu.CompilerParams(vmem_limit_bytes=VMEM_BYTES),
        cost_estimate=pl.CostEstimate(
            flops=1 << 20, bytes_accessed=7 * MICROSECOND, transcendentals=0
        ),
        name="exit_product",
    )(hidden, *values)


def combine_kernel(slot_ref, length_ref, tokens_ref, attended_ref, gate_ref, *refs):
    out_ref = refs[-1]
    present = lax.broadcasted_iota(jnp.int32, gate_ref.shape, 0) < length_ref[0]
    summed = jnp.concatenate([ref[...] for ref in refs[:-1]], axis=1).astype(F32)
    accept = 1.0 / (1.0 + jnp.exp(-gate_ref[...]))
    middle = (tokens_ref[...].astype(F32) + attended_ref[...].astype(F32)).astype(BF16)
    combined = middle.astype(F32) + accept * summed
    out_ref[...] = jnp.where(present, combined, 0.0).astype(BF16)


def combine(slot, length, tokens, attended, gate, summed):
    seq_len, wide = gate.shape
    whole = pl.BlockSpec((seq_len, wide), lambda i, *_: (0, 0))
    parts = [pl.BlockSpec(part.shape, lambda i, *_: (0, 0)) for part in summed]
    return pl.pallas_call(
        combine_kernel,
        grid_spec=pltpu.PrefetchScalarGridSpec(
            num_scalar_prefetch=2,
            grid=(1,),
            in_specs=[pl.BlockSpec((seq_len, wide), lambda i, slot, *_: (0, slot[0]))] * 2
            + [whole]
            + parts,
            out_specs=whole,
        ),
        out_shape=jax.ShapeDtypeStruct((seq_len, wide), BF16),
        compiler_params=pltpu.CompilerParams(vmem_limit_bytes=VMEM_BYTES),
        cost_estimate=pl.CostEstimate(
            flops=1 << 20, bytes_accessed=3 * MICROSECOND, transcendentals=0
        ),
        name="combine",
    )(slot, length, tokens, attended, gate, *summed)


def local(
    input_activations,
    prompt_extents,
    continuing_flags,
    owning_index,
    partition_arrangement,
    training_accept_pieces,
    training_lookup_pieces,
    training_content_pieces,
    normalizer_scales,
    prior_step_blends,
    forgetting_bias_vector,
    forgetting_left_lowrank,
    forgetting_right_lowrank,
    instant_emphasis,
    group_normalizer_scale,
    gating_projection,
    mixing_exit_projection,
    kept_summary_places,
    previous_normed_entries,
    feedforward_entry_proj,
    feedforward_exit_proj,
    feedforward_accept_proj,
):
    hid = lax.axis_size("hid")
    req = lax.axis_size("req")
    here = lax.axis_index("req")
    slot = lax.axis_index("hid")
    token_rows = input_activations[0]
    seq_len, width = token_rows.shape
    local_width = mixing_exit_projection.shape[0]
    heads = local_width // GROUP_DIMENSION
    shards = partition_arrangement.shape[0]
    shard_rows = width // shards
    length = prompt_extents[0]
    resuming = continuing_flags[0]

    owned = (resuming == 1) & (owning_index[0] == slot)
    saved = jnp.where(owned, kept_summary_places[0, 0].astype(BF16), 0)
    start = lax.psum_scatter(
        saved.reshape(saved.shape[0], -1), "hid", scatter_dimension=0, tiled=True
    )
    start = start.astype(F32).reshape(heads, GROUP_DIMENSION, GROUP_DIMENSION)

    order = jnp.concatenate(
        [
            lax.dynamic_slice_in_dim(partition_arrangement, (here ^ d) * hid, hid, 0)
            for d in range(req)
        ]
    )
    gain_rows = normalizer_scales.astype(F32)
    mix_rows = prior_step_blends.astype(F32)
    carried = jnp.where(resuming == 1, previous_normed_entries[0].astype(F32), 0.0)
    if shard_rows % 128 == 0:
        blended, decay_in, gate_in, last_in = prepare(
            order, prompt_extents, token_rows, gain_rows[:1], carried[:1], mix_rows[:5]
        )
    else:
        normed_in = layer_norm(token_rows.astype(F32), gain_rows[0])
        before = shifted(normed_in, carried[0])
        rec_in, key_in, val_in, decay_in, gate_in = [
            (normed_in + (before - normed_in) * mix_rows[m][None, :]).astype(BF16)
            for m in range(5)
        ]
        blended = jnp.stack([rec_in, key_in, val_in]).reshape(3, seq_len, shards, shard_rows)
        blended = jnp.take(blended, order, axis=2).reshape(3, seq_len, width)
        last_in = lax.dynamic_slice_in_dim(normed_in, length - 1, 1, 0)

    def side_products(decay_in, gate_in):
        low_rank = jnp.tanh(matmul(decay_in, forgetting_left_lowrank)).astype(BF16)
        return matmul(low_rank, forgetting_right_lowrank), matmul(gate_in, gating_projection)

    def to_heads(columns):
        mine = lax.all_to_all(columns, "hid", split_axis=0, concat_axis=0, tiled=True)
        mine = mine.reshape(hid, -1, shard_rows, local_width)
        return [mine[: hid // 2], mine[hid // 2 :]]

    columns = regroup(
        [training_accept_pieces, training_lookup_pieces, training_content_pieces], hid
    )
    units = feedforward_entry_proj.shape[0]
    hold = lax.optimization_barrier
    if req == 4:
        half = units // 2
        cut = half * 11 // 14 // 16 * 16
        key_mine, value_mine = feedforward_entry_proj, feedforward_exit_proj
        key_x, key_y = across(key_mine, 1), across(key_mine, 2)
        mine = to_heads(columns)
        decay, gate = side_products(decay_in, gate_in)
        mine, key_x, key_y, blended, decay, gate, start = hold(
            (mine, key_x, key_y, blended, decay, gate, start)
        )
        trained = [mine, [across(rows, 1) for rows in mine], [across(rows, 2) for rows in mine]]
        first = [key_x[:cut], key_y[half : half + cut]]
        second = [key_x[cut:half], key_y[half + cut :]]
        trained, first, second = hold((trained, first, second))
        opposite = [across(trained[1][0], 2), across(trained[2][1], 1)]
        projected = project(blended, sum(trained, []))
        projected, opposite, first = hold((projected, opposite, first))
        key_far = [across(first[0], 2), across(first[1], 1)]
    else:
        decay, gate = side_products(decay_in, gate_in)
        low, high = [whole(side, req) for side in to_heads(columns)]
        opposite = []
        projected = project(blended, [side[d] for d in range(req) for side in (low, high)])
    head_terms, new_state = recurrence(
        prompt_extents,
        projected,
        blended,
        opposite,
        decay,
        gate,
        forgetting_bias_vector[None],
        instant_emphasis[None],
        group_normalizer_scale[None],
        start,
        mixing_exit_projection,
    )
    attended = lax.psum(head_terms, "hid")
    if req == 4:
        new_state, value_mine, second, key_far = hold((new_state, value_mine, second, key_far))
        value_x, value_y = across(value_mine, 1), across(value_mine, 2)
        key_far.insert(1, across(second[0], 2))
        key_far.append(across(second[1], 1))
        value_far = [value_x[:half], value_y[half:]]
        value_far, key_far = hold((value_far, key_far))
        value_far = [across(value_far[0], 2), across(value_far[1], 1)]
        key_rows = [key_mine, key_x, key_y, *key_far]
        value_rows = [value_mine, value_x, value_y, *value_far]
    else:
        key_rows = whole(feedforward_entry_proj, req)
        value_rows = whole(feedforward_exit_proj, req)
    hidden, accept_in, last_chan = channel_inputs(
        prompt_extents,
        token_rows,
        attended,
        gain_rows[1:],
        carried[1:],
        mix_rows[5:],
        key_rows,
    )
    accept = matmul(accept_in, feedforward_accept_proj)
    terms = exit_product(hidden, value_rows)
    summed = lax.psum_scatter(terms, "hid", scatter_dimension=1, tiled=True)
    layer_out = combine(
        slot[None], prompt_extents, token_rows, attended, accept, [summed]
    )[None]
    shift_out = jnp.concatenate([last_in, last_chan]).astype(BF16)[None]
    return (layer_out, new_state[None], shift_out)


def solution(mesh):
    placed = (
        P("req", None, None),
        P("req"),
        P("req"),
        P("req"),
        P(),
        P(("req", "hid"), None),
        P(("req", "hid"), None),
        P(("req", "hid"), None),
        P(),
        P(),
        P("hid"),
        P(),
        P(None, "hid"),
        P("hid"),
        P("hid"),
        P(None, "hid"),
        P("hid", None),
        P("req", "hid", None, None, None),
        P("req", None, None),
        P(("req", "hid"), None),
        P(("req", "hid"), None),
        P(None, "hid"),
    )
    return jax.shard_map(
        local,
        mesh=mesh,
        in_specs=placed,
        out_specs=(P("req", None, "hid"), P("req", "hid", None, None), P("req", None, None)),
        check_vma=False,
    )
```

```python
from functools import partial

import jax
import jax.numpy as jnp
from jax import lax
from jax.experimental import pallas as pl
from jax.experimental.pallas import tpu as pltpu
from jax.sharding import PartitionSpec as P

GROUP_DIMENSION = 64
PAIR = 2 * GROUP_DIMENSION
CHUNK = 64
BF16 = jnp.bfloat16
F32 = jnp.float32
MICROSECOND = 3690000
VMEM_BYTES = 60 << 20


def layer_norm(values, gain):
    center = values - jnp.mean(values, axis=-1, keepdims=True)
    spread = jnp.mean(center * center, axis=-1, keepdims=True)
    return center / jnp.sqrt(spread + 1e-05) * gain


def shifted(values, first_row):
    return jnp.concatenate([first_row[None, :], values[:-1]], axis=0)


def matmul(a, b):
    return jnp.dot(a, b, preferred_element_type=F32)


def matmul_nt(a, b):
    return lax.dot_general(a, b, (((1,), (1,)), ((), ())), preferred_element_type=F32)


def matmul_tn(a, b):
    return lax.dot_general(a, b, (((0,), (0,)), ((), ())), preferred_element_type=F32)


def across(value, axis):
    return lax.ppermute(value, "req", [(i, i ^ axis) for i in range(4)])


def whole(value, req):
    blocks = lax.all_gather(value, "req", axis=0, tiled=False)
    me = lax.axis_index("req")
    return [lax.dynamic_index_in_dim(blocks, me ^ d, 0, keepdims=False) for d in range(req)]


def by_head(values, first_lanes):
    zeros = jnp.zeros_like(values)
    return jnp.concatenate(
        [jnp.where(first_lanes, values, zeros), jnp.where(first_lanes, zeros, values)], axis=0
    )


def split_matmul(values, weights):
    high = values.astype(BF16)
    low = (values - high.astype(F32)).astype(BF16)
    return matmul(high, weights) + matmul(low, weights)


def recurrence_kernel(
    steps,
    count,
    length_ref,
    base_ref,
    values_ref,
    *refs,
):
    rows_far, refs = refs[:count], refs[count:]
    decay_ref, gate_ref, bias_ref, bonus_ref, gain_ref, start_ref, exit_ref = refs[:7]
    terms_ref, state_ref, held, projected, gated_ref, total_ref = refs[7:]
    rec_ref, key_ref, val_ref = (projected.at[m] for m in range(3))
    for m in range(3):
        projected[m] = rows_product(base_ref[m], values_ref, m, rows_far)
    length = length_ref[0]
    tokens = base_ref.shape[1]
    size = min(CHUNK, tokens)
    lanes = lax.broadcasted_iota(jnp.int32, (size, PAIR), 1)
    first_lanes = lanes < GROUP_DIMENSION
    row_of = lax.broadcasted_iota(jnp.int32, (size, PAIR), 0)
    t_of = lax.broadcasted_iota(jnp.int32, (size, 2 * size), 0)
    s_of = lax.broadcasted_iota(jnp.int32, (size, 2 * size), 1) & (size - 1)
    side_a = lax.broadcasted_iota(jnp.int32, (PAIR, PAIR), 0) < GROUP_DIMENSION
    side_b = lax.broadcasted_iota(jnp.int32, (PAIR, PAIR), 1) < GROUP_DIMENSION
    own_head = side_a == side_b
    average = jnp.where(own_head, 1.0 / GROUP_DIMENSION, 0.0).astype(BF16)
    pairs_here = base_ref.shape[2] // PAIR
    for pair in range(pairs_here):
        start = start_ref[2 * pair : 2 * pair + 2].reshape(PAIR, GROUP_DIMENSION)
        start = jnp.where(own_head, jnp.concatenate([start, start], axis=1), 0.0)
        held[pair] = start.T
    for index, pair in [(i, p) for i in range(tokens // size) for p in range(pairs_here)]:
        rows = (pl.ds(index * size, size), pl.ds(pair * PAIR, PAIR))
        bias, bonus, gain = (ref[:, rows[1]] for ref in (bias_ref, bonus_ref, gain_ref))
        present = row_of + index * size < length
        rec = rec_ref[rows]
        key = jnp.where(present, key_ref[rows], 0.0)
        val = val_ref[rows].astype(BF16)
        total = jnp.where(present, -jnp.exp(bias + decay_ref[rows]), 0.0)
        scores = jnp.where(
            t_of == s_of,
            matmul_nt((rec * bonus).astype(BF16), by_head(key.astype(BF16), first_lanes)),
            0.0,
        )
        before = jnp.zeros_like(total)
        after = jnp.zeros_like(total)
        span = 1
        while span < size:
            later = (row_of & span) != 0
            scaled = (jnp.where(later, rec, key) * jnp.exp(jnp.where(later, before, after))).astype(
                BF16
            )
            pairs = matmul_nt(scaled, by_head(scaled, first_lanes))
            chosen = (
                ((t_of & span) != 0)
                & ((s_of & span) == 0)
                & ((t_of & (-2 * span)) == (s_of & (-2 * span)))
            )
            scores = jnp.where(chosen, pairs, scores)
            partner = jnp.where(
                later, pltpu.roll(total, span, 0), pltpu.roll(total, size - span, 0)
            )
            before = before + jnp.where(later, partner, 0.0)
            after = after + jnp.where(later, 0.0, partner)
            total = total + partner
            span *= 2
        state = held[pair]
        out = matmul(scores.astype(BF16), by_head(val, first_lanes))
        out = out + matmul_nt((rec * jnp.exp(before)).astype(BF16), state.astype(BF16))
        update = matmul_tn(val, (key * jnp.exp(after)).astype(BF16))
        held[pair] = state * jnp.exp(total[:1, :]) + jnp.where(own_head, update, 0.0)
        center = out - split_matmul(out, average)
        spread = split_matmul(center * center, average)
        grouped = center * lax.rsqrt(spread + 0.00064) * gain
        gate = gate_ref[rows]
        gated_ref[rows] = (grouped * (gate / (1.0 + jnp.exp(-gate)))).astype(BF16)
    for pair in range(pairs_here):
        final = held[pair].T
        final = final[:, :GROUP_DIMENSION] + final[:, GROUP_DIMENSION:]
        state_ref[2 * pair : 2 * pair + 2] = final.reshape(2, GROUP_DIMENSION, GROUP_DIMENSION)
    step = pl.program_id(0)
    width = exit_ref.shape[1]
    tile = min(1024, width)
    for first in range(0, width, tile):
        columns = slice(first, first + tile)
        part = matmul(gated_ref[...], exit_ref[:, columns])
        if steps == 1:
            terms_ref[:, columns] = part.astype(BF16)
            continue

        @pl.when(step == 0)
        def _():
            total_ref[:, columns] = part

        @pl.when((step > 0) & (step < steps - 1))
        def _():
            total_ref[:, columns] += part

        @pl.when(step == steps - 1)
        def _():
            terms_ref[:, columns] = (total_ref[:, columns] + part).astype(BF16)


def recurrence(length, base, values, far, decay, gate, bias, bonus, gain, start, exit_rows):
    tokens, width = decay.shape
    out_width = exit_rows.shape[1]
    together = min(2, width // PAIR)
    lanes = together * PAIR
    steps = width // lanes
    reach = sum(r.shape[0] * r.shape[2] for r in far) or 128
    place = values.shape[2] // reach - 1
    wide = pl.BlockSpec((tokens, lanes), lambda p: (0, p))
    row = pl.BlockSpec((1, lanes), lambda p: (0, p))
    states = pl.BlockSpec((2 * together, GROUP_DIMENSION, GROUP_DIMENSION), lambda p: (p, 0, 0))
    return pl.pallas_call(
        partial(recurrence_kernel, steps, len(far)),
        grid=(steps,),
        in_specs=[
            pl.BlockSpec(memory_space=pltpu.SMEM),
            pl.BlockSpec((3, tokens, lanes), lambda p: (0, 0, p)),
            pl.BlockSpec((3, tokens, reach), lambda p: (0, 0, place)),
        ]
        + [pl.BlockSpec((*r.shape[:3], lanes), lambda p: (0, 0, 0, p)) for r in far]
        + [wide] * 2
        + [row] * 3
        + [states, pl.BlockSpec((lanes, out_width), lambda p: (p, 0))],
        out_specs=[pl.BlockSpec((tokens, out_width), lambda p: (0, 0)), states],
        out_shape=[
            jax.ShapeDtypeStruct((tokens, out_width), BF16),
            jax.ShapeDtypeStruct(start.shape, F32),
        ],
        scratch_shapes=[
            pltpu.VMEM((together, PAIR, PAIR), F32),
            pltpu.VMEM((3, tokens, lanes), F32),
            pltpu.VMEM((tokens, lanes), BF16),
            pltpu.VMEM((tokens, out_width), F32),
        ],
        compiler_params=pltpu.CompilerParams(vmem_limit_bytes=44 << 20),
        cost_estimate=pl.CostEstimate(
            flops=1 << 20, bytes_accessed=24 * MICROSECOND, transcendentals=0
        ),
        name="recurrence",
    )(length, base, values, *far, decay, gate, bias, bonus, gain, start, exit_rows)


def prepare_kernel(
    order_ref,
    length_ref,
    tokens_ref,
    gain_ref,
    first_ref,
    mix_ref,
    stack_ref,
    out3_ref,
    out4_ref,
    last_ref,
    mean_ref,
    root_ref,
):
    step = pl.program_id(0)
    block = out3_ref.shape[1]
    seq_len, width = tokens_ref.shape

    @pl.when(step == 0)
    def _():
        count = min(64, seq_len)
        for index in range(seq_len // count):
            rows = pl.ds(index * count, count)
            values = tokens_ref[rows, :].astype(F32)
            mean = jnp.mean(values, axis=1, keepdims=True)
            center = values - mean
            spread = jnp.mean(center * center, axis=1, keepdims=True)
            mean_ref[rows, :] = jnp.broadcast_to(mean, (count, 128))
            root_ref[rows, :] = jnp.broadcast_to(lax.rsqrt(spread + 1e-05), (count, 128))

    columns = pl.ds(pl.multiple_of(order_ref[step] * block, block), block)
    values = tokens_ref[:, columns].astype(F32)
    normed = (values - mean_ref[:, :1]) * root_ref[:, :1] * gain_ref[:1, columns]
    places = lax.broadcasted_iota(jnp.int32, normed.shape, 0)
    before = jnp.where(places == 0, first_ref[:1, columns], pltpu.roll(normed, 1, 0))
    change = before - normed
    outs = [stack_ref.at[0], stack_ref.at[1], stack_ref.at[2], out3_ref, out4_ref]
    for m, out_ref in enumerate(outs):
        out_ref[...] = (normed + change * mix_ref[m : m + 1, columns]).astype(BF16)
    last = places == length_ref[0] - 1
    last_ref[...] = jnp.sum(jnp.where(last, normed, 0.0), axis=0, keepdims=True)


def prepare(order, length, tokens, gain, first, mixes):
    seq_len, width = tokens.shape
    blocks = order.shape[0]
    block = width // blocks

    def rows(count):
        return pl.BlockSpec((count, width), lambda j, *_: (0, 0))

    moved = pl.BlockSpec((3, seq_len, block), lambda j, *_: (0, 0, j))
    natural = pl.BlockSpec((seq_len, block), lambda j, order, *_: (0, order[j]))
    return pl.pallas_call(
        prepare_kernel,
        grid_spec=pltpu.PrefetchScalarGridSpec(
            num_scalar_prefetch=2,
            grid=(blocks,),
            in_specs=[rows(seq_len), rows(1), rows(1), rows(mixes.shape[0])],
            out_specs=[moved]
            + [natural] * 2
            + [pl.BlockSpec((1, block), lambda j, order, *_: (0, order[j]))],
            scratch_shapes=[pltpu.VMEM((seq_len, 128), F32)] * 2,
        ),
        out_shape=[jax.ShapeDtypeStruct((3, seq_len, width), BF16)]
        + [jax.ShapeDtypeStruct((seq_len, width), BF16)] * 2
        + [jax.ShapeDtypeStruct((1, width), F32)],
        compiler_params=pltpu.CompilerParams(vmem_limit_bytes=VMEM_BYTES),
        cost_estimate=pl.CostEstimate(
            flops=1 << 20, bytes_accessed=22 * MICROSECOND, transcendentals=0
        ),
        name="prepare",
    )(order, length, tokens, gain, first, mixes)


def regroup_kernel(*refs):
    out_ref = refs[-1]
    rows = refs[0].shape[0]
    count, _, wide = out_ref.shape
    for at, piece_ref in enumerate(refs[:-1]):
        for h in range(count):
            block = piece_ref[:, h * wide : (h + 1) * wide]
            out_ref[h, at * rows : (at + 1) * rows, :] = block.astype(BF16)


def regroup(pieces, hid):
    rows, width = pieces[0].shape
    wide = width // hid
    tall = rows * len(pieces)
    steps = 4
    return pl.pallas_call(
        regroup_kernel,
        grid=(steps,),
        in_specs=[pl.BlockSpec((rows, width // steps), lambda h: (0, h))] * len(pieces),
        out_specs=pl.BlockSpec((hid // steps, tall, wide), lambda h: (h, 0, 0)),
        out_shape=jax.ShapeDtypeStruct((hid, tall, wide), BF16),
        compiler_params=pltpu.CompilerParams(vmem_limit_bytes=VMEM_BYTES),
        cost_estimate=pl.CostEstimate(flops=0, bytes_accessed=20 << 20, transcendentals=0),
        name="regroup",
    )(*pieces)


def rows_product(total, values_ref, m, rows):
    first = 0
    for rows_ref in rows:
        block = rows_ref[:, m]
        span = block.shape[0] * block.shape[1]
        values = values_ref[m, :, first : first + span]
        total = total + matmul(values, block.reshape(span, block.shape[2]))
        first += span
    return total


def project_kernel(values_ref, *refs):
    refs[-1][0] = rows_product(0.0, values_ref, 0, refs[:-1])


def project(values, rows):
    count, tokens, width = values.shape
    wide = rows[0].shape[-1]
    tile = min(256, wide)
    out = pl.BlockSpec((1, tokens, tile), lambda m, n: (m, 0, n))
    return pl.pallas_call(
        project_kernel,
        grid=(count, wide // tile),
        in_specs=[pl.BlockSpec((1, tokens, width), lambda m, n: (m, 0, 0))]
        + [
            pl.BlockSpec((r.shape[0], 1, r.shape[2], tile), lambda m, n: (0, m, 0, n))
            for r in rows
        ],
        out_specs=out,
        out_shape=jax.ShapeDtypeStruct((count, tokens, wide), F32),
        compiler_params=pltpu.CompilerParams(vmem_limit_bytes=VMEM_BYTES),
        cost_estimate=pl.CostEstimate(
            flops=1 << 20, bytes_accessed=13 * MICROSECOND, transcendentals=0
        ),
        name="project",
    )(values, *rows)


def channel_kernel(places, steps, length_ref, tokens_ref, attended_ref, gain_ref, first_ref, mix_ref, *refs):
    count = len(places)
    rows, refs = refs[:count], refs[count:]
    hidden_ref, accept_ref, last_ref, held, mixed, taken, arrived = refs
    step = pl.program_id(0)
    copies = [
        pltpu.make_async_copy(ref, taken.at[pl.ds(first, ref.shape[0]), :], arrived.at[at])
        for at, (ref, first) in enumerate(zip(rows, places))
    ]

    @pl.when(step == 0)
    def _():
        for copy in copies:
            copy.start()
        held[...] = first_ref[...]
        last_ref[...] = jnp.zeros_like(last_ref)

    middle = (tokens_ref[...].astype(F32) + attended_ref[...].astype(F32)).astype(BF16)
    values = middle.astype(F32)
    center = values - jnp.mean(values, axis=1, keepdims=True)
    spread = jnp.mean(center * center, axis=1, keepdims=True)
    normed = center * lax.rsqrt(spread + 1e-05) * gain_ref[...]
    tall = normed.shape[0]
    row_of = lax.broadcasted_iota(jnp.int32, normed.shape, 0)
    before = jnp.where(row_of == 0, held[...], pltpu.roll(normed, 1, 0))
    held[...] = normed[tall - 1 :, :]
    change = before - normed
    mixed[pl.ds(pl.multiple_of(step * tall, tall), tall), :] = (
        normed + change * mix_ref[:1, :]
    ).astype(BF16)
    accept_ref[...] = (normed + change * mix_ref[1:2, :]).astype(BF16)
    place = length_ref[0] - 1 - step * tall

    @pl.when((place >= 0) & (place < tall))
    def _():
        last_ref[...] = jnp.sum(jnp.where(row_of == place, normed, 0.0), axis=0, keepdims=True)

    @pl.when(step == steps - 1)
    def _():
        units = hidden_ref.shape[1]
        ready = 0
        for first in range(0, units, 256):
            end = min(first + 256, units)
            while ready < count and places[ready] < end:
                copies[ready].wait()
                ready += 1
            inner = jnp.maximum(matmul_nt(mixed[...], taken[first:end, :]), 0.0)
            hidden_ref[:, first:end] = (inner * inner).astype(BF16)


def channel_inputs(length, tokens, attended, gain, first, mixes, rows):
    seq_len, width = tokens.shape
    tall = min(128, seq_len)
    steps = seq_len // tall
    by_rows = pl.BlockSpec((tall, width), lambda i: (i, 0))
    places = [0]
    for block in rows:
        places.append(places[-1] + block.shape[0])

    def wide(number):
        return pl.BlockSpec((number, width), lambda i: (0, 0))

    return pl.pallas_call(
        partial(channel_kernel, places[:-1], steps),
        grid=(steps,),
        in_specs=[
            pl.BlockSpec(memory_space=pltpu.SMEM),
            by_rows,
            by_rows,
            wide(1),
            wide(1),
            wide(2),
        ]
        + [pl.BlockSpec(memory_space=pl.ANY)] * len(rows),
        out_specs=[
            pl.BlockSpec((seq_len, places[-1]), lambda i: (0, 0)),
            by_rows,
            wide(1),
        ],
        out_shape=[
            jax.ShapeDtypeStruct((seq_len, places[-1]), BF16),
            jax.ShapeDtypeStruct((seq_len, width), BF16),
            jax.ShapeDtypeStruct((1, width), F32),
        ],
        scratch_shapes=[
            pltpu.VMEM((1, width), F32),
            pltpu.VMEM((seq_len, width), BF16),
            pltpu.VMEM((places[-1], width), BF16),
            pltpu.SemaphoreType.DMA((len(rows),)),
        ],
        compiler_params=pltpu.CompilerParams(vmem_limit_bytes=VMEM_BYTES),
        cost_estimate=pl.CostEstimate(
            flops=1 << 20, bytes_accessed=22 * MICROSECOND, transcendentals=0
        ),
        name="channel_inputs",
    )(length, tokens, attended, gain, first, mixes, *rows)


def exit_kernel(hidden_ref, *refs):
    values = jnp.concatenate([ref[...] for ref in refs[:-1]], axis=0)
    refs[-1][...] = matmul(hidden_ref[...], values).astype(BF16)


def exit_product(hidden, values):
    tokens = hidden.shape[0]
    width = values[0].shape[1]
    tile = min(1024, width)
    return pl.pallas_call(
        exit_kernel,
        grid=(width // tile,),
        in_specs=[pl.BlockSpec(hidden.shape, lambda n: (0, 0))]
        + [pl.BlockSpec((v.shape[0], tile), lambda n: (0, n)) for v in values],
        out_specs=pl.BlockSpec((tokens, tile), lambda n: (0, n)),
        out_shape=jax.ShapeDtypeStruct((tokens, width), BF16),
        compiler_params=pltpu.CompilerParams(vmem_limit_bytes=VMEM_BYTES),
        cost_estimate=pl.CostEstimate(
            flops=1 << 20, bytes_accessed=7 * MICROSECOND, transcendentals=0
        ),
        name="exit_product",
    )(hidden, *values)


def local(
    input_activations,
    prompt_extents,
    continuing_flags,
    owning_index,
    partition_arrangement,
    training_accept_pieces,
    training_lookup_pieces,
    training_content_pieces,
    normalizer_scales,
    prior_step_blends,
    forgetting_bias_vector,
    forgetting_left_lowrank,
    forgetting_right_lowrank,
    instant_emphasis,
    group_normalizer_scale,
    gating_projection,
    mixing_exit_projection,
    kept_summary_places,
    previous_normed_entries,
    feedforward_entry_proj,
    feedforward_exit_proj,
    feedforward_accept_proj,
):
    hid = lax.axis_size("hid")
    req = lax.axis_size("req")
    here = lax.axis_index("req")
    slot = lax.axis_index("hid")
    token_rows = input_activations[0]
    seq_len, width = token_rows.shape
    local_width = mixing_exit_projection.shape[0]
    heads = local_width // GROUP_DIMENSION
    shards = partition_arrangement.shape[0]
    shard_rows = width // shards
    length = prompt_extents[0]
    resuming = continuing_flags[0]

    owned = (resuming == 1) & (owning_index[0] == slot)
    saved = jnp.where(owned, kept_summary_places[0, 0].astype(BF16), 0)
    start = lax.psum_scatter(
        saved.reshape(saved.shape[0], -1), "hid", scatter_dimension=0, tiled=True
    )
    start = start.astype(F32).reshape(heads, GROUP_DIMENSION, GROUP_DIMENSION)

    order = jnp.concatenate(
        [
            lax.dynamic_slice_in_dim(partition_arrangement, (here ^ d) * hid, hid, 0)
            for d in range(req)
        ]
    )
    gain_rows = normalizer_scales.astype(F32)
    mix_rows = prior_step_blends.astype(F32)
    carried = jnp.where(resuming == 1, previous_normed_entries[0].astype(F32), 0.0)
    if shard_rows % 128 == 0:
        blended, decay_in, gate_in, last_in = prepare(
            order, prompt_extents, token_rows, gain_rows[:1], carried[:1], mix_rows[:5]
        )
    else:
        normed_in = layer_norm(token_rows.astype(F32), gain_rows[0])
        before = shifted(normed_in, carried[0])
        rec_in, key_in, val_in, decay_in, gate_in = [
            (normed_in + (before - normed_in) * mix_rows[m][None, :]).astype(BF16)
            for m in range(5)
        ]
        blended = jnp.stack([rec_in, key_in, val_in]).reshape(3, seq_len, shards, shard_rows)
        blended = jnp.take(blended, order, axis=2).reshape(3, seq_len, width)
        last_in = lax.dynamic_slice_in_dim(normed_in, length - 1, 1, 0)

    def side_products(decay_in, gate_in):
        low_rank = jnp.tanh(matmul(decay_in, forgetting_left_lowrank)).astype(BF16)
        return matmul(low_rank, forgetting_right_lowrank), matmul(gate_in, gating_projection)

    def to_heads(columns):
        mine = lax.all_to_all(columns, "hid", split_axis=0, concat_axis=0, tiled=True)
        mine = mine.reshape(hid, -1, shard_rows, local_width)
        return [mine[: hid // 2], mine[hid // 2 :]]

    columns = regroup(
        [training_accept_pieces, training_lookup_pieces, training_content_pieces], hid
    )
    units = feedforward_entry_proj.shape[0]
    hold = lax.optimization_barrier
    if req == 4:
        half = units // 2
        cut = half * 11 // 14 // 16 * 16
        key_mine, value_mine = feedforward_entry_proj, feedforward_exit_proj
        key_x, key_y = across(key_mine, 1), across(key_mine, 2)
        mine = to_heads(columns)
        decay, gate = side_products(decay_in, gate_in)
        mine, key_x, key_y, blended, decay, gate, start = hold(
            (mine, key_x, key_y, blended, decay, gate, start)
        )
        trained = [mine, [across(rows, 1) for rows in mine], [across(rows, 2) for rows in mine]]
        first = [key_x[:cut], key_y[half : half + cut]]
        second = [key_x[cut:half], key_y[half + cut :]]
        trained, first, second = hold((trained, first, second))
        opposite = [across(trained[1][0], 2), across(trained[2][1], 1)]
        projected = project(blended, sum(trained, []))
        projected, opposite, first = hold((projected, opposite, first))
        key_far = [across(first[0], 2), across(first[1], 1)]
    else:
        decay, gate = side_products(decay_in, gate_in)
        low, high = [whole(side, req) for side in to_heads(columns)]
        opposite = []
        projected = project(blended, [side[d] for d in range(req) for side in (low, high)])
    head_terms, new_state = recurrence(
        prompt_extents,
        projected,
        blended,
        opposite,
        decay,
        gate,
        forgetting_bias_vector[None],
        instant_emphasis[None],
        group_normalizer_scale[None],
        start,
        mixing_exit_projection,
    )
    attended = lax.psum(head_terms, "hid")
    if req == 4:
        new_state, value_mine, second, key_far = hold((new_state, value_mine, second, key_far))
        value_x, value_y = across(value_mine, 1), across(value_mine, 2)
        key_far.insert(1, across(second[0], 2))
        key_far.append(across(second[1], 1))
        value_far = [value_x[:half], value_y[half:]]
        value_far, key_far = hold((value_far, key_far))
        value_far = [across(value_far[0], 2), across(value_far[1], 1)]
        key_rows = [key_mine, key_x, key_y, *key_far]
        value_rows = [value_mine, value_x, value_y, *value_far]
    else:
        key_rows = whole(feedforward_entry_proj, req)
        value_rows = whole(feedforward_exit_proj, req)
    hidden, accept_in, last_chan = channel_inputs(
        prompt_extents,
        token_rows,
        attended,
        gain_rows[1:],
        carried[1:],
        mix_rows[5:],
        key_rows,
    )
    accept = matmul(accept_in, feedforward_accept_proj)
    terms = exit_product(hidden, value_rows)
    summed = lax.psum_scatter(terms, "hid", scatter_dimension=1, tiled=True)
    present = (jnp.arange(seq_len) < length)[:, None]
    first_column = slot * local_width
    middle = lax.dynamic_slice_in_dim(token_rows, first_column, local_width, 1).astype(F32)
    middle += lax.dynamic_slice_in_dim(attended, first_column, local_width, 1).astype(F32)
    middle = jnp.where(present, middle.astype(BF16), 0)
    accept = jnp.where(present, jax.nn.sigmoid(accept), 0.0)
    middle, accept = hold((middle, accept))
    layer_out = (middle.astype(F32) + accept * summed.astype(F32)).astype(BF16)[None]
    shift_out = jnp.concatenate([last_in, last_chan]).astype(BF16)[None]
    return (layer_out, new_state[None], shift_out)


def solution(mesh):
    placed = (
        P("req", None, None),
        P("req"),
        P("req"),
        P("req"),
        P(),
        P(("req", "hid"), None),
        P(("req", "hid"), None),
        P(("req", "hid"), None),
        P(),
        P(),
        P("hid"),
        P(),
        P(None, "hid"),
        P("hid"),
        P("hid"),
        P(None, "hid"),
        P("hid", None),
        P("req", "hid", None, None, None),
        P("req", None, None),
        P(("req", "hid"), None),
        P(("req", "hid"), None),
        P(None, "hid"),
    )
    return jax.shard_map(
        local,
        mesh=mesh,
        in_specs=placed,
        out_specs=(P("req", None, "hid"), P("req", "hid", None, None), P("req", None, None)),
        check_vma=False,
    )
```
